512 devices in a mesh: ctx: 64 (over z, y_lo, core), head: 8 (over x, y_hi).
Axes of the slice: x: 4, y: 8 (y_hi: 2, y_lo: 4; y = y_hi * 4 + y_lo), z: 8, core: 2. Of those that a mesh axis runs over, the one named last changes fastest.
Arguments:
- queries: bfloat16 [65536, 4096], P('ctx', 'head'), may hold values from -5 to 5
- keys: bfloat16 [65536, 1024], P('ctx', 'head'), may hold values from -5 to 5
- values: bfloat16 [65536, 1024], P('ctx', 'head'), may hold values from -16 to 16
- d_attn: bfloat16 [65536, 4096], P('ctx', 'head'), may hold values from -16 to 16
- inputs: bfloat16 [65536, 4096], P('ctx', 'head'), may hold values from -6 to 6
- random_ids: int32 [1024, 3], replicated, may hold values from 0 to 1023, as said below
- global_ids: int32 [2], replicated, may hold values from 0 to 1023
- step_codes: int32 [2], replicated, may hold values from 0 to 999
- momentum: float32 [8, 256, 256], P('head', 'ctx'), may hold values from -6 to 6
Outputs:
- d_queries: bfloat16 [65536, 4096], P('ctx', 'head')
- new_momentum: float32 [8, 256, 256], P('head', 'ctx')
- weight_step: float32 [8, 256, 4096], P('head', 'ctx')
The draws below stay inside these ranges and needn't reach their ends.
Inputs may be any that keep to these rules, and one draw needn't show every extreme that they name: `random_ids`: row b names the random key blocks of query block b. In the rows of one device of ctx (aligned runs of 16 rows), at most 2 entries name blocks of any one device (blocks c * 16 to (c + 1) * 16 - 1), a block named twice counting twice, and in the rows of every device some device is named exactly 2 times.
All inputs are finite; a program needn't handle non-finite values.
Results may differ from the reference program's by a relative error of at most 0.027.
Values may be sent and summed in bfloat16 or wider, within the bound.
No kernel may reach another device: no remote copies, remote signals or barrier semaphores. Data moves between devices by JAX's collectives and lax.ppermute only.
A program may use at most 128 MiB of HBM per device.

```python
import math
import jax
import jax.numpy as jnp
from jax import lax

D = 4096
HEAD_SIZE = 128
GROUP = 4
KVH = 8
QH = 32
BLK = 64
RAND = 3
GLOB = 2
RANK = 256
TOK_DEV = 1024
SEQ = 65536
NB = 1024
CAP = 2
N_CTX = 64


def draw_queries(key, part):
    base = jnp.clip(jax.random.normal(jax.random.fold_in(key, 41), (SEQ, QH * HEAD_SIZE)), -4.0, 4.0)
    return base.astype(jnp.bfloat16)


def draw_keys(key, part):
    base = jnp.clip(jax.random.normal(jax.random.fold_in(key, 42), (SEQ, KVH * HEAD_SIZE)), -4.0, 4.0)
    return base.astype(jnp.bfloat16)


def draw_random_ids(key, part):
    per_dev = TOK_DEV // BLK
    requests = per_dev * RAND
    owner_keys = jax.random.split(jax.random.fold_in(key, 21), N_CTX)
    owner_perms = jax.vmap(lambda one_key: jax.random.permutation(one_key, N_CTX))(owner_keys)
    slot_pos = jnp.arange(requests, dtype=jnp.int32) // CAP % N_CTX
    owners = owner_perms[:, slot_pos]
    local_ids = jax.random.randint(jax.random.fold_in(key, 22), (N_CTX, requests), 0, per_dev)
    order_keys = jax.random.split(jax.random.fold_in(key, 23), N_CTX)
    orders = jax.vmap(lambda one_key: jax.random.permutation(one_key, requests))(order_keys)
    block_ids = owners * per_dev + local_ids
    block_ids = jnp.take_along_axis(block_ids, orders, axis=1)
    return block_ids.reshape(NB, RAND).astype(jnp.int32)


def block_levels(stream_key, shape, shards, least, largest):
    gain = 1.0
    for position, blocks in shards:
        heights = jax.random.uniform(jax.random.fold_in(jax.random.fold_in(stream_key, 6), position), (blocks,), jnp.float32, least / len(shards), largest / len(shards))
        gain = gain * jnp.repeat(jnp.exp(heights), shape[position] // blocks).reshape((-1,) + (1,) * (len(shape) - 1 - position))
    return gain


def noise(stream_key, extent, width, bound, pieces=(), held_as=jnp.bfloat16):
    entries = width * jax.random.normal(stream_key, extent, jnp.float32)
    if pieces:
        entries = entries * block_levels(stream_key, extent, pieces, -0.22, 0.18)
    return jnp.clip(entries, -bound, bound).astype(held_as)


def setup_inputs(seed: int = 0) -> dict:
    key_of = jax.random.split(jax.random.key(seed), 10)
    queries = draw_queries(jax.random.fold_in(key_of[9], 71), 0)
    keys = draw_keys(jax.random.fold_in(key_of[9], 71), 0)
    values = noise(key_of[2], (SEQ, KVH * HEAD_SIZE), 4.0, 16.0, ((0, 64), (1, 8)))
    d_attn = noise(key_of[3], (SEQ, QH * HEAD_SIZE), 4.0, 16.0, ((0, 64), (1, 8)))
    inputs = noise(key_of[4], (SEQ, D), 1.0, 6.0, ((0, 64), (1, 8)))
    random_ids = draw_random_ids(jax.random.fold_in(key_of[9], 71), 0)
    global_ids = jax.random.randint(key_of[6], (GLOB,), 0, NB).astype(jnp.int32)
    step_codes = jax.random.randint(key_of[7], (2,), 0, 1000).astype(jnp.int32)
    momentum = noise(key_of[8], (KVH, 2 * HEAD_SIZE, RANK), 1.0, 6.0, ((0, 8), (1, 64)), jnp.float32)
    return dict(queries=queries, keys=keys, values=values, d_attn=d_attn, inputs=inputs, random_ids=random_ids, global_ids=global_ids, step_codes=step_codes, momentum=momentum)


def proj_table(code_value, rank_ids, feature_ids):
    row_ids = rank_ids[:, None]
    col_ids = feature_ids[None, :]
    section_one = (row_ids * 31337 + col_ids * 7919 + code_value * 10007) % 65521
    section_two = (section_one * 181 + section_one % 251 * 4093 + col_ids) % 65521
    section_three = (section_two * (section_two % 127 + 1) + row_ids * 17) % 65521
    unit_value = (section_three.astype(jnp.float32) + 0.5) / 65521.0 - 0.5
    return (unit_value * math.sqrt(12.0 / D)).astype(jnp.bfloat16)

def reference(queries, keys, values, d_attn, inputs, random_ids, global_ids, step_codes, momentum):
    scaling = 1.0 / math.sqrt(HEAD_SIZE)
    highest = lax.Precision.HIGHEST
    rank_ids = jnp.arange(RANK, dtype=jnp.int32)
    feature_ids = jnp.arange(D, dtype=jnp.int32)
    table_new = proj_table(step_codes[1], rank_ids, feature_ids)
    table_old = proj_table(step_codes[0], rank_ids, feature_ids)
    projected = jnp.dot(inputs, table_new.T, preferred_element_type=jnp.float32).astype(jnp.bfloat16)
    key_blocks = keys.reshape(NB, BLK, KVH, HEAD_SIZE)
    value_blocks = values.reshape(NB, BLK, KVH, HEAD_SIZE)
    projection_blocks = projected.reshape(NB, BLK, RANK)
    query_blocks = queries.reshape(NB, BLK, KVH, GROUP, HEAD_SIZE)
    grad_blocks = d_attn.reshape(NB, BLK, KVH, GROUP, HEAD_SIZE)

    def group_stride(totals, block_id):
        key_grad, value_grad = totals
        neighbours = jnp.stack([block_id - 1, block_id, block_id + 1]).astype(jnp.int32)
        chosen_rand = lax.dynamic_index_in_dim(random_ids, block_id, 0, keepdims=False).astype(jnp.int32)
        listed = jnp.concatenate([neighbours, chosen_rand, global_ids.astype(jnp.int32)])
        slot_valid = jnp.concatenate([jnp.stack([block_id > 0, block_id >= 0, block_id < NB - 1]), jnp.ones((RAND + GLOB,), bool)])
        listed = jnp.clip(listed, 0, NB - 1)
        slot_keys = key_blocks[listed].reshape(-1, KVH, HEAD_SIZE).astype(jnp.float32)
        slot_values = value_blocks[listed].reshape(-1, KVH, HEAD_SIZE).astype(jnp.float32)
        slot_proj = projection_blocks[listed].reshape(-1, RANK).astype(jnp.float32)
        key_ok = jnp.repeat(slot_valid, BLK)
        query_row_span = lax.dynamic_index_in_dim(query_blocks, block_id, 0, keepdims=False).astype(jnp.float32)
        grad_rows = lax.dynamic_index_in_dim(grad_blocks, block_id, 0, keepdims=False).astype(jnp.float32)
        scores = jnp.einsum('qgjd,kgd->gjqk', query_row_span, slot_keys, precision=highest) * scaling
        scores = jnp.where(key_ok, scores, -1e+30)
        row_max = lax.optimization_barrier(jnp.max(scores, axis=-1, keepdims=True))
        exponent = jnp.exp(scores - row_max)
        weights = exponent / lax.optimization_barrier(jnp.sum(exponent, axis=-1, keepdims=True))
        weights_bf = lax.optimization_barrier(weights.astype(jnp.bfloat16)).astype(jnp.float32)
        attention = jnp.einsum('gjqk,kgd->qgjd', weights_bf, slot_values, precision=highest).astype(jnp.bfloat16)
        carried = jnp.einsum('gjqk,kr->gjqr', weights_bf, slot_proj, precision=highest)
        attention_f = lax.optimization_barrier(attention).astype(jnp.float32)
        row_delta = jnp.transpose(lax.optimization_barrier(jnp.sum(grad_rows * attention_f, axis=-1)), (1, 2, 0))
        d_weights = jnp.einsum('qgjd,kgd->gjqk', grad_rows, slot_values, precision=highest)
        d_scores = lax.optimization_barrier((weights * (d_weights - row_delta[..., None])).astype(jnp.bfloat16)).astype(jnp.float32)
        d_query = (jnp.einsum('gjqk,kgd->qgjd', d_scores, slot_keys, precision=highest) * scaling).astype(jnp.bfloat16)
        proj_back = jnp.einsum('gjqk,kr->gjqr', d_scores, slot_proj, precision=highest)
        key_grad = key_grad + jnp.einsum('qgjd,gjqr->gdr', query_row_span, proj_back, precision=highest) * scaling
        value_grad = value_grad + jnp.einsum('qgjd,gjqr->gdr', grad_rows, carried, precision=highest)
        return ((key_grad, value_grad), d_query)
    start = (jnp.zeros((KVH, HEAD_SIZE, RANK), jnp.float32), jnp.zeros((KVH, HEAD_SIZE, RANK), jnp.float32))
    (key_grad, value_grad), dq_blocks = lax.scan(group_stride, start, jnp.arange(NB, dtype=jnp.int32))
    gradient = jnp.concatenate([key_grad, value_grad], axis=1) / math.sqrt(SEQ)
    expanded = jnp.einsum('grk,kd->grd', momentum, table_old.astype(jnp.float32), precision=highest)
    carried_back = jnp.einsum('grd,kd->grk', expanded, table_new.astype(jnp.float32), precision=highest)
    new_momentum = 0.9 * carried_back + gradient
    weight_step = jnp.einsum('grk,kd->grd', new_momentum, table_new.astype(jnp.float32), precision=highest)
    return (dq_blocks.reshape(SEQ, QH * HEAD_SIZE), new_momentum, weight_step)
```

```python
import functools
import math

import jax
import jax.numpy as jnp
from jax import lax
from jax.experimental import pallas as pl
from jax.experimental.pallas import tpu as pltpu
from jax.sharding import PartitionSpec as P

D = 4096
HEAD_SIZE = 128
GROUP = 4
BLK = 64
RAND = 3
GLOB = 2
RANK = 256
CAP = 2
ROWS = 16
PARTS = BLK // ROWS
LIMIT = 48 * 1024 * 1024
F32 = jnp.float32
BF16 = jnp.bfloat16
VMEM = pl.BlockSpec(memory_space=pltpu.VMEM)
SMEM = pl.BlockSpec(memory_space=pltpu.SMEM)
PARAMS = pltpu.CompilerParams(vmem_limit_bytes=LIMIT)


def proj_table(code_value, rank_ids, feature_ids):
    row_ids = rank_ids[:, None]
    col_ids = feature_ids[None, :]
    section_one = (row_ids * 31337 + col_ids * 7919 + code_value * 10007) % 65521
    section_two = (section_one * 181 + section_one % 251 * 4093 + col_ids) % 65521
    section_three = (section_two * (section_two % 127 + 1) + row_ids * 17) % 65521
    unit_value = (section_three.astype(jnp.float32) + 0.5) / 65521.0 - 0.5
    return (unit_value * math.sqrt(12.0 / D)).astype(jnp.bfloat16)


def dot(a, b, da, db):
    return lax.dot_general(a, b, (((da,), (db,)), ((), ())), preferred_element_type=F32)


def split3(x):
    high = x.astype(BF16)
    rest = x - high.astype(F32)
    mid = rest.astype(BF16)
    return high, mid, (rest - mid.astype(F32)).astype(BF16)


def pack_kv(src_ref, k_ref, v_ref, out_ref):
    here = out_ref.shape[0]
    first = pl.program_id(0) * here
    for i in range(here):
        rows = pl.ds(pl.multiple_of(src_ref[first + i] * BLK, BLK), BLK)
        out_ref[i, :, :HEAD_SIZE] = k_ref[rows, :]
        out_ref[i, :, HEAD_SIZE:] = v_ref[rows, :]


def project(x_ref, t_ref, out_ref):
    blocks = out_ref.shape[1]
    y = dot(x_ref[...], t_ref[...], 1, 1).astype(out_ref.dtype)
    for b in range(blocks):
        for part in range(PARTS):
            row = b * BLK + part * ROWS
            for half in range(2):
                out_ref[half * PARTS + part, b] = y[row : row + ROWS, half * 128 : half * 128 + 128]


def sum_pack(src_ref, gid_ref, x_ref, own_ref, out_ref, acc):
    own = x_ref[0].astype(F32)
    for i in range(1, x_ref.shape[0]):
        own = own + x_ref[i].astype(F32)
    acc[...] = own.astype(BF16)
    own_ref[...] = acc[...]
    for i in range(out_ref.shape[0]):
        for c in range(CAP):
            out_ref[i, c] = acc[src_ref[i * CAP + c]]
        for g in range(GLOB):
            out_ref[i, CAP + g] = acc[gid_ref[g]]


def collect(arrival_ref, owner_ref, own_ref, before_ref, after_ref, recv_ref, out_ref):
    blocks = own_ref.shape[0]
    tiles = [before_ref[...]] + [own_ref[b] for b in range(blocks)] + [after_ref[...]]
    tiles += [recv_ref[owner_ref[g] * (CAP + GLOB) + CAP + g] for g in range(GLOB)]
    tiles += [recv_ref[arrival_ref[n] // CAP * (CAP + GLOB) + arrival_ref[n] % CAP] for n in range(blocks * RAND)]
    for n, tile in enumerate(tiles):
        for h in range(out_ref.shape[0]):
            out_ref[h, n] = tile


def attend(
    arrival_ref, edge_ref, q_ref, g_ref, k_ref, v_ref, before_ref, after_ref, glob_ref, recv_ref,
    dq_ref, kg_ref, kwin, vwin, wacc, gacc,
):
    step, steps = pl.program_id(0), pl.num_programs(0)
    tokens = k_ref.shape[0]
    blocks = tokens // BLK
    unroll = q_ref.shape[0] // BLK
    scaling = 1.0 / math.sqrt(HEAD_SIZE)
    h = HEAD_SIZE

    @pl.when(step == 0)
    def _():
        for win, ref, low in ((kwin, k_ref, 0), (vwin, v_ref, h)):
            win[:BLK] = before_ref[:, low : low + h]
            win[BLK : BLK + tokens] = ref[...]
            win[BLK + tokens :] = after_ref[:, low : low + h]
        wacc[...] = jnp.zeros_like(wacc)
        gacc[...] = jnp.zeros_like(gacc)

    for u in range(unroll):
        b = step * unroll + u
        rows = pl.ds(pl.multiple_of(b * BLK, BLK), 3 * BLK)
        picks = [arrival_ref[b * RAND + r] for r in range(RAND)]
        k_all = jnp.concatenate([kwin[rows, :]] + [recv_ref[p, :, :h] for p in picks] + [glob_ref[:, :h]], axis=0)
        v_all = jnp.concatenate([vwin[rows, :]] + [recv_ref[p, :, h:] for p in picks] + [glob_ref[:, h:]], axis=0)
        here = slice(u * BLK, (u + 1) * BLK)
        q = jnp.concatenate([q_ref[here, j * h : (j + 1) * h] for j in range(GROUP)], axis=0)
        g = jnp.concatenate([g_ref[here, j * h : (j + 1) * h] for j in range(GROUP)], axis=0)
        s = dot(k_all, q, 1, 1) * (scaling * math.log2(math.e))
        left = jnp.where(b == 0, edge_ref[0], 0).astype(F32) * -1e30
        right = jnp.where(b == blocks - 1, edge_ref[1], 0).astype(F32) * -1e30
        s = jnp.concatenate(
            [s[:BLK] + left, s[BLK : 2 * BLK], s[2 * BLK : 3 * BLK] + right, s[3 * BLK :]], axis=0
        )
        e = jnp.exp2(s - jnp.max(s, axis=0, keepdims=True))
        w = e * (1.0 / jnp.sum(e, axis=0, keepdims=True))
        w_bf = w.astype(BF16)
        dw = dot(v_all, g, 1, 1)
        delta = jnp.sum(w_bf.astype(F32) * dw, axis=0, keepdims=True)
        ds = (w * (dw - delta)).astype(BF16)
        dq = jnp.transpose(dot(k_all, ds, 0, 0) * scaling).astype(BF16)
        for j in range(GROUP):
            dq_ref[here, j * h : (j + 1) * h] = dq[j * BLK : (j + 1) * BLK]
        kg = dot(ds, q, 1, 0) * scaling
        vg = dot(w_bf, g, 1, 0)
        wacc[rows, :h] += kg[: 3 * BLK]
        wacc[rows, h:] += vg[: 3 * BLK]
        gacc[:, :h] += kg[(3 + RAND) * BLK :]
        gacc[:, h:] += vg[(3 + RAND) * BLK :]
        for r in range(RAND):
            for part in range(PARTS):
                low = (3 + r) * BLK + part * ROWS
                place = blocks + 2 + GLOB + b * RAND + r
                kg_ref[part, place, :, :h] = kg[low : low + ROWS].astype(BF16)
                kg_ref[part, place, :, h:] = vg[low : low + ROWS].astype(BF16)

    @pl.when(step == steps - 1)
    def _():
        for acc, first, count in ((wacc, 0, blocks + 2), (gacc, blocks + 2, GLOB)):
            for n in range(count):
                for part in range(PARTS):
                    low = n * BLK + part * ROWS
                    kg_ref[part, first + n] = acc[low : low + ROWS, :].astype(BF16)


def gradient(kg_ref, p_ref, out_ref, acc):
    step = pl.program_id(0)
    terms = jnp.concatenate([dot(kg_ref[0], p_ref[i, 0], 0, 0) for i in range(2)], axis=1)

    @pl.when(step == 0)
    def _():
        acc[...] = terms

    @pl.when(step > 0)
    def _():
        acc[...] += terms

    @pl.when(step == pl.num_programs(0) - 1)
    def _():
        out_ref[...] = acc[...]


def carry(m_ref, old_ref, new_ref, out_ref):
    rows = m_ref.shape[0]
    x = dot(jnp.concatenate(split3(m_ref[...]), axis=0), old_ref[...], 1, 0)
    x = x[:rows] + x[rows : 2 * rows] + x[2 * rows :]
    y = dot(jnp.concatenate(split3(x), axis=0), new_ref[...], 1, 1)
    out_ref[...] = 0.9 * (y[:rows] + y[rows : 2 * rows] + y[2 * rows :])


def finish(scale, recv_ref, carried_ref, new_ref, mom_ref, step_ref):
    rows = mom_ref.shape[0]
    total = carried_ref[:rows] + jnp.sum(recv_ref[...], axis=0) * scale
    mom_ref[...] = total
    padded = jnp.concatenate([total, jnp.zeros((8 - rows, RANK), F32)], axis=0)
    y = dot(jnp.concatenate(split3(padded), axis=0), new_ref[...], 1, 0)
    step_ref[...] = (y[:8] + y[8:16] + y[16:])[:rows]


def local(queries, keys, values, d_attn, inputs, random_ids, global_ids, step_codes, momentum):
    tokens = queries.shape[0]
    blocks = tokens // BLK
    ctx, heads = lax.axis_size("ctx"), lax.axis_size("head")
    my_ctx, my_head = lax.axis_index("ctx"), lax.axis_index("head")
    requests = blocks * RAND
    places = blocks + 2 + GLOB + requests
    h = HEAD_SIZE
    up = [(i, i + 1) for i in range(ctx - 1)]
    down = [(i + 1, i) for i in range(ctx - 1)]

    ids = random_ids.reshape(ctx, requests)
    owners, inner = ids // blocks, ids % blocks
    order = jnp.arange(requests, dtype=jnp.int32)
    tagged = order[None, :] * blocks + inner
    mine = owners == my_ctx
    first = jnp.min(jnp.where(mine, tagged, requests * blocks), axis=1) % blocks
    last = jnp.max(jnp.where(mine, tagged, 0), axis=1) % blocks
    sources = jnp.stack([first, last], axis=1).reshape(-1)
    my_owners = lax.dynamic_index_in_dim(owners, my_ctx, 0, keepdims=False)
    earlier = (my_owners[:, None] == my_owners[None, :]) & (order[None, :] < order[:, None])
    arrival = my_owners * CAP + jnp.any(earlier, axis=1).astype(jnp.int32)
    global_owner, global_inner = global_ids // blocks, global_ids % blocks

    chunk = 16
    kv_out = pl.pallas_call(
        pack_kv,
        grid_spec=pltpu.PrefetchScalarGridSpec(
            num_scalar_prefetch=1,
            grid=(ctx * CAP // chunk,),
            in_specs=[VMEM, VMEM],
            out_specs=pl.BlockSpec((chunk, BLK, 2 * h), lambda i, s: (i, 0, 0)),
        ),
        out_shape=jax.ShapeDtypeStruct((ctx * CAP, BLK, 2 * h), BF16),
        compiler_params=PARAMS,
    )(sources, keys, values)
    kv_in = lax.all_to_all(kv_out.reshape(ctx, CAP, BLK, 2 * h), "ctx", 0, 0, tiled=True)
    kv_in = kv_in.reshape(ctx * CAP, BLK, 2 * h)

    feature_ids = my_head * inputs.shape[1] + jnp.arange(inputs.shape[1], dtype=jnp.int32)
    rank_ids = jnp.arange(RANK, dtype=jnp.int32)
    table_part = proj_table(step_codes[1], rank_ids, feature_ids)
    terms = pl.pallas_call(
        project,
        in_specs=[VMEM] * 2,
        out_specs=VMEM,
        out_shape=jax.ShapeDtypeStruct((heads, blocks, ROWS, 128), BF16),
        compiler_params=PARAMS,
    )(inputs, table_part)
    terms = lax.all_to_all(terms, "head", 0, 0, tiled=True)
    own, p_out = pl.pallas_call(
        sum_pack,
        in_specs=[SMEM, SMEM, VMEM],
        out_specs=[VMEM] * 2,
        out_shape=[
            jax.ShapeDtypeStruct((blocks, ROWS, 128), BF16),
            jax.ShapeDtypeStruct((ctx, CAP + GLOB, ROWS, 128), BF16),
        ],
        scratch_shapes=[pltpu.VMEM((blocks, ROWS, 128), BF16)],
        compiler_params=PARAMS,
    )(sources, global_inner, terms)

    kv_before = lax.ppermute(jnp.concatenate([keys[-BLK:], values[-BLK:]], axis=1), "ctx", up)
    kv_after = lax.ppermute(jnp.concatenate([keys[:BLK], values[:BLK]], axis=1), "ctx", down)
    p_before = lax.ppermute(own[-1], "ctx", up)
    p_after = lax.ppermute(own[0], "ctx", down)
    kv_glob = []
    for g in range(GLOB):
        row = global_inner[g] * BLK
        kv_glob.append(jnp.concatenate([lax.dynamic_slice_in_dim(x, row, BLK, 0) for x in (keys, values)], axis=1))
    kv_glob = jnp.stack(kv_glob)
    apart = my_ctx ^ global_owner
    bit = 1
    while bit < ctx:
        other = lax.ppermute(kv_glob, "ctx", [(i, i ^ bit) for i in range(ctx)])
        kv_glob = jnp.where(((apart & bit) != 0)[:, None, None], other, kv_glob)
        bit *= 2
    kv_glob = kv_glob.reshape(GLOB * BLK, 2 * h)

    p_in = lax.all_to_all(p_out, "ctx", 0, 0, tiled=True)
    tiles = pl.pallas_call(
        collect,
        in_specs=[SMEM, SMEM] + [VMEM] * 4,
        out_specs=VMEM,
        out_shape=jax.ShapeDtypeStruct((heads, places, ROWS, 128), BF16),
        compiler_params=PARAMS,
    )(arrival, global_owner, own, p_before, p_after, p_in.reshape(ctx * (CAP + GLOB), ROWS, 128))
    tiles = lax.all_to_all(tiles, "head", 0, 0, tiled=True)

    every = jnp.arange(D, dtype=jnp.int32)
    table_new = proj_table(step_codes[1], rank_ids, every)
    table_old = proj_table(step_codes[0], rank_ids, every)
    share = momentum.shape[1]
    carried = pl.pallas_call(
        carry,
        in_specs=[VMEM] * 3,
        out_specs=VMEM,
        out_shape=jax.ShapeDtypeStruct((8, RANK), F32),
        compiler_params=PARAMS,
    )(jnp.pad(momentum[0], ((0, 8 - share), (0, 0))), table_old, table_new)

    edges = jnp.stack([my_ctx == 0, my_ctx == ctx - 1]).astype(jnp.int32)
    unroll = 2
    wide = pl.BlockSpec((unroll * BLK, GROUP * h), lambda i: (i, 0))
    dq, grads = pl.pallas_call(
        attend,
        grid=(blocks // unroll,),
        in_specs=[SMEM, SMEM, wide, wide] + [VMEM] * 6,
        out_specs=[wide, VMEM],
        out_shape=[
            jax.ShapeDtypeStruct((tokens, GROUP * h), BF16),
            jax.ShapeDtypeStruct((PARTS, places, ROWS, 2 * h), BF16),
        ],
        scratch_shapes=[
            pltpu.VMEM((tokens + 2 * BLK, h), BF16),
            pltpu.VMEM((tokens + 2 * BLK, h), BF16),
            pltpu.VMEM((tokens + 2 * BLK, 2 * h), F32),
            pltpu.VMEM((GLOB * BLK, 2 * h), F32),
        ],
        compiler_params=PARAMS,
    )(arrival, edges, queries, d_attn, keys, values, kv_before, kv_after, kv_glob, kv_in)

    grad = pl.pallas_call(
        gradient,
        grid=(PARTS,),
        in_specs=[
            pl.BlockSpec((1, places * ROWS, 2 * h), lambda i: (i, 0, 0)),
            pl.BlockSpec((2, 1, places * ROWS, 128), lambda i: (0, i, 0, 0)),
        ],
        out_specs=pl.BlockSpec((2 * h, RANK), lambda i: (0, 0)),
        out_shape=jax.ShapeDtypeStruct((2 * h, RANK), F32),
        scratch_shapes=[pltpu.VMEM((2 * h, RANK), F32)],
        compiler_params=PARAMS,
    )(grads.reshape(PARTS, places * ROWS, 2 * h), tiles.reshape(2, PARTS, places * ROWS, 128))
    grad = lax.all_to_all(grad.reshape(ctx, share, RANK), "ctx", 0, 0, tiled=True)
    new_momentum, weight_step = pl.pallas_call(
        functools.partial(finish, 1.0 / math.sqrt(tokens * ctx)),
        in_specs=[VMEM] * 3,
        out_specs=[VMEM] * 2,
        out_shape=[
            jax.ShapeDtypeStruct((share, RANK), F32),
            jax.ShapeDtypeStruct((share, D), F32),
        ],
        compiler_params=PARAMS,
    )(grad, carried, table_new)
    return dq, new_momentum[None], weight_step[None]


def solution(mesh):
    in_specs = (
        P("ctx", "head"),
        P("ctx", "head"),
        P("ctx", "head"),
        P("ctx", "head"),
        P("ctx", "head"),
        P(),
        P(),
        P(),
        P("head", "ctx", None),
    )
    out_specs = (P("ctx", "head"), P("head", "ctx", None), P("head", "ctx", None))
    return jax.shard_map(local, mesh=mesh, in_specs=in_specs, out_specs=out_specs, check_vma=False)
```

```python
import functools
import math

import jax
import jax.numpy as jnp
from jax import lax
from jax.experimental import pallas as pl
from jax.experimental.pallas import tpu as pltpu
from jax.sharding import PartitionSpec as P

D = 4096
HEAD_SIZE = 128
GROUP = 4
BLK = 64
RAND = 3
GLOB = 2
RANK = 256
CAP = 2
ROWS = 16
PARTS = BLK // ROWS
F32 = jnp.float32
BF16 = jnp.bfloat16
VMEM = pl.BlockSpec(memory_space=pltpu.VMEM)
ANY = pl.BlockSpec(memory_space=pl.ANY)
SMEM = pl.BlockSpec(memory_space=pltpu.SMEM)
PARAMS = pltpu.CompilerParams(vmem_limit_bytes=16 * 1024 * 1024)
LARGE = pltpu.CompilerParams(vmem_limit_bytes=30 * 1024 * 1024)


def proj_table(code_value, rank_ids, feature_ids):
    row_ids = rank_ids[:, None]
    col_ids = feature_ids[None, :]
    section_one = (row_ids * 31337 + col_ids * 7919 + code_value * 10007) % 65521
    section_two = (section_one * 181 + section_one % 251 * 4093 + col_ids) % 65521
    section_three = (section_two * (section_two % 127 + 1) + row_ids * 17) % 65521
    unit_value = (section_three.astype(jnp.float32) + 0.5) / 65521.0 - 0.5
    return (unit_value * math.sqrt(12.0 / D)).astype(jnp.bfloat16)


def dot(a, b, da, db):
    return lax.dot_general(a, b, (((da,), (db,)), ((), ())), preferred_element_type=F32)


def split3(x):
    high = x.astype(BF16)
    rest = x - high.astype(F32)
    mid = rest.astype(BF16)
    return high, mid, (rest - mid.astype(F32)).astype(BF16)


def pack_kv(src_ref, k_ref, v_ref, out_ref):
    here = out_ref.shape[0]
    first = pl.program_id(0) * here
    for i in range(here):
        rows = pl.ds(pl.multiple_of(src_ref[first + i] * BLK, BLK), BLK)
        out_ref[i, :, :HEAD_SIZE] = k_ref[rows, :]
        out_ref[i, :, HEAD_SIZE:] = v_ref[rows, :]


def project(x_ref, t_ref, out_ref):
    blocks = out_ref.shape[1]
    y = dot(x_ref[...], t_ref[...], 1, 1).astype(out_ref.dtype)
    for b in range(blocks):
        for part in range(PARTS):
            row = b * BLK + part * ROWS
            for half in range(2):
                out_ref[half * PARTS + part, b] = y[row : row + ROWS, half * 128 : half * 128 + 128]


def sum_pack(src_ref, gid_ref, x_ref, own_ref, out_ref, acc):
    own = x_ref[0].astype(F32)
    for i in range(1, x_ref.shape[0]):
        own = own + x_ref[i].astype(F32)
    acc[...] = own.astype(BF16)
    own_ref[...] = acc[...]
    for i in range(out_ref.shape[0]):
        for c in range(CAP):
            out_ref[i, c] = acc[src_ref[i * CAP + c]]
        for g in range(GLOB):
            out_ref[i, CAP + g] = acc[gid_ref[g]]


def collect(arrival_ref, owner_ref, own_ref, before_ref, after_ref, recv_ref, out_ref):
    blocks = own_ref.shape[0]
    tiles = [before_ref[...]] + [own_ref[b] for b in range(blocks)] + [after_ref[...]]
    tiles += [recv_ref[owner_ref[g] * (CAP + GLOB) + CAP + g] for g in range(GLOB)]
    tiles += [recv_ref[arrival_ref[n] // CAP * (CAP + GLOB) + arrival_ref[n] % CAP] for n in range(blocks * RAND)]
    for n, tile in enumerate(tiles):
        out_ref[n] = tile


def attend(
    arrival_ref, edge_ref, from_ref, q_ref, g_ref, k_ref, v_ref, before_ref, after_ref, glob_ref, recv_ref, *refs
):
    dq_ref, out_ref, kwin, vwin, wacc, gacc, kg_ref, total = refs[-8:]
    tile_refs = refs[:-10]
    step, steps = pl.program_id(0), pl.num_programs(0)
    tokens = k_ref.shape[0]
    blocks = tokens // BLK
    unroll = q_ref.shape[0] // BLK
    scaling = 1.0 / math.sqrt(HEAD_SIZE)
    h = HEAD_SIZE

    @pl.when(step == 0)
    def _():
        for win, ref, low in ((kwin, k_ref, 0), (vwin, v_ref, h)):
            win[:BLK] = before_ref[:, low : low + h]
            win[BLK : BLK + tokens] = ref[...]
            win[BLK + tokens :] = after_ref[:, low : low + h]
        wacc[...] = jnp.zeros_like(wacc)
        gacc[...] = jnp.zeros_like(gacc)

    for u in range(unroll):
        b = step * unroll + u
        rows = pl.ds(pl.multiple_of(b * BLK, BLK), 3 * BLK)
        picks = [arrival_ref[b * RAND + r] for r in range(RAND)]
        k_all = jnp.concatenate([kwin[rows, :]] + [recv_ref[p, :, :h] for p in picks] + [glob_ref[:, :h]], axis=0)
        v_all = jnp.concatenate([vwin[rows, :]] + [recv_ref[p, :, h:] for p in picks] + [glob_ref[:, h:]], axis=0)
        here = slice(u * BLK, (u + 1) * BLK)
        q = jnp.concatenate([q_ref[here, j * h : (j + 1) * h] for j in range(GROUP)], axis=0)
        g = jnp.concatenate([g_ref[here, j * h : (j + 1) * h] for j in range(GROUP)], axis=0)
        s = dot(k_all, q, 1, 1) * (scaling * math.log2(math.e))
        left = jnp.where(b == 0, edge_ref[0], 0).astype(F32) * -1e30
        right = jnp.where(b == blocks - 1, edge_ref[1], 0).astype(F32) * -1e30
        s = jnp.concatenate(
            [s[:BLK] + left, s[BLK : 2 * BLK], s[2 * BLK : 3 * BLK] + right, s[3 * BLK :]], axis=0
        )
        e = jnp.exp2(s - jnp.max(s, axis=0, keepdims=True))
        w = e * (1.0 / jnp.sum(e, axis=0, keepdims=True))
        w_bf = w.astype(BF16)
        dw = dot(v_all, g, 1, 1)
        delta = jnp.sum(w_bf.astype(F32) * dw, axis=0, keepdims=True)
        ds = (w * (dw - delta)).astype(BF16)
        dq = jnp.transpose(dot(k_all, ds, 0, 0) * scaling).astype(BF16)
        for j in range(GROUP):
            dq_ref[here, j * h : (j + 1) * h] = dq[j * BLK : (j + 1) * BLK]
        kg = dot(ds, q, 1, 0) * scaling
        vg = dot(w_bf, g, 1, 0)
        wacc[rows, :h] += kg[: 3 * BLK]
        wacc[rows, h:] += vg[: 3 * BLK]
        gacc[:, :h] += kg[(3 + RAND) * BLK :]
        gacc[:, h:] += vg[(3 + RAND) * BLK :]
        for r in range(RAND):
            for part in range(PARTS):
                low = (3 + r) * BLK + part * ROWS
                place = blocks + 2 + GLOB + b * RAND + r
                kg_ref[part, place, :, :h] = kg[low : low + ROWS].astype(BF16)
                kg_ref[part, place, :, h:] = vg[low : low + ROWS].astype(BF16)

    @pl.when(step == steps - 1)
    def _():
        for acc, first, count in ((wacc, 0, blocks + 2), (gacc, blocks + 2, GLOB)):
            for n in range(count):
                for part in range(PARTS):
                    low = n * BLK + part * ROWS
                    kg_ref[part, first + n] = acc[low : low + ROWS, :].astype(BF16)
        total[...] = jnp.zeros_like(total)
        many = kg_ref.shape[1] * ROWS
        for i, ref in enumerate(tile_refs):
            head = from_ref[i]
            kg = kg_ref[head % PARTS].reshape(many, 2 * h)
            total[head // PARTS] += dot(kg, ref[...].reshape(many, 128), 0, 0)
        rows = total.shape[1] // out_ref.shape[0]
        for d in range(out_ref.shape[0]):
            for half in range(2):
                out_ref[d, half * rows : (half + 1) * rows] = total[half, d * rows : (d + 1) * rows]


def carry(m_ref, old_ref, new_ref, out_ref):
    rows = m_ref.shape[0]
    x = dot(jnp.concatenate(split3(m_ref[...]), axis=0), old_ref[...], 1, 0)
    x = x[:rows] + x[rows : 2 * rows] + x[2 * rows :]
    y = dot(jnp.concatenate(split3(x), axis=0), new_ref[...], 1, 1)
    out_ref[...] = 0.9 * (y[:rows] + y[rows : 2 * rows] + y[2 * rows :])


def finish(scale, recv_ref, carried_ref, new_ref, mom_ref, step_ref):
    rows = mom_ref.shape[0]
    grad = jnp.sum(recv_ref[...], axis=0) * scale
    total = carried_ref[:rows] + jnp.concatenate([grad[:rows], grad[rows:]], axis=1)
    mom_ref[...] = total
    padded = jnp.concatenate([total, jnp.zeros((8 - rows, RANK), F32)], axis=0)
    y = dot(jnp.concatenate(split3(padded), axis=0), new_ref[...], 1, 0)
    step_ref[...] = (y[:8] + y[8:16] + y[16:])[:rows]


def local(queries, keys, values, d_attn, inputs, random_ids, global_ids, step_codes, momentum):
    tokens = queries.shape[0]
    blocks = tokens // BLK
    ctx, heads = lax.axis_size("ctx"), lax.axis_size("head")
    my_ctx, my_head = lax.axis_index("ctx"), lax.axis_index("head")
    requests = blocks * RAND
    places = blocks + 2 + GLOB + requests
    h = HEAD_SIZE
    up = [(i, i + 1) for i in range(ctx - 1)]
    down = [(i + 1, i) for i in range(ctx - 1)]

    ids = random_ids.reshape(ctx, requests)
    owners, inner = ids // blocks, ids % blocks
    order = jnp.arange(requests, dtype=jnp.int32)
    tagged = order[None, :] * blocks + inner
    mine = owners == my_ctx
    first = jnp.min(jnp.where(mine, tagged, requests * blocks), axis=1) % blocks
    last = jnp.max(jnp.where(mine, tagged, 0), axis=1) % blocks
    sources = jnp.stack([first, last], axis=1).reshape(-1)
    my_owners = lax.dynamic_index_in_dim(owners, my_ctx, 0, keepdims=False)
    earlier = (my_owners[:, None] == my_owners[None, :]) & (order[None, :] < order[:, None])
    arrival = my_owners * CAP + jnp.any(earlier, axis=1).astype(jnp.int32)
    global_owner, global_inner = global_ids // blocks, global_ids % blocks

    feature_ids = my_head * inputs.shape[1] + jnp.arange(inputs.shape[1], dtype=jnp.int32)
    rank_ids = jnp.arange(RANK, dtype=jnp.int32)
    table_part = proj_table(step_codes[1], rank_ids, feature_ids)
    terms = pl.pallas_call(
        project,
        in_specs=[VMEM] * 2,
        out_specs=VMEM,
        out_shape=jax.ShapeDtypeStruct((heads, blocks, ROWS, 128), BF16),
        compiler_params=PARAMS,
    )(inputs, table_part)
    terms = lax.all_to_all(terms, "head", 0, 0, tiled=True)
    own, p_out = pl.pallas_call(
        sum_pack,
        in_specs=[SMEM, SMEM, VMEM],
        out_specs=[VMEM] * 2,
        out_shape=[
            jax.ShapeDtypeStruct((blocks, ROWS, 128), BF16),
            jax.ShapeDtypeStruct((ctx, CAP + GLOB, ROWS, 128), BF16),
        ],
        scratch_shapes=[pltpu.VMEM((blocks, ROWS, 128), BF16)],
        compiler_params=PARAMS,
    )(sources, global_inner, terms)

    kv_before = lax.ppermute(jnp.concatenate([keys[-BLK:], values[-BLK:]], axis=1), "ctx", up)
    kv_after = lax.ppermute(jnp.concatenate([keys[:BLK], values[:BLK]], axis=1), "ctx", down)
    p_before = lax.ppermute(own[-1], "ctx", up)
    p_after = lax.ppermute(own[0], "ctx", down)
    kv_glob = []
    for g in range(GLOB):
        row = global_inner[g] * BLK
        kv_glob.append(jnp.concatenate([lax.dynamic_slice_in_dim(x, row, BLK, 0) for x in (keys, values)], axis=1))
    kv_glob = jnp.stack(kv_glob)
    apart = my_ctx ^ global_owner
    bit = 1
    while bit < ctx:
        other = lax.ppermute(kv_glob, "ctx", [(i, i ^ bit) for i in range(ctx)])
        kv_glob = jnp.where(((apart & bit) != 0)[:, None, None], other, kv_glob)
        bit *= 2
    kv_glob = kv_glob.reshape(GLOB * BLK, 2 * h)

    p_in = lax.all_to_all(p_out, "ctx", 0, 0, tiled=True)
    tiles = pl.pallas_call(
        collect,
        in_specs=[SMEM, SMEM] + [VMEM] * 4,
        out_specs=VMEM,
        out_shape=jax.ShapeDtypeStruct((places, ROWS, 128), BF16),
        compiler_params=PARAMS,
    )(arrival, global_owner, own, p_before, p_after, p_in.reshape(ctx * (CAP + GLOB), ROWS, 128))
    pair = [tiles, lax.ppermute(tiles, "head", [(i, i ^ 1) for i in range(heads)])]
    chunk = 16
    kv_out = pl.pallas_call(
        pack_kv,
        grid_spec=pltpu.PrefetchScalarGridSpec(
            num_scalar_prefetch=1,
            grid=(ctx * CAP // chunk,),
            in_specs=[VMEM, VMEM],
            out_specs=pl.BlockSpec((chunk, BLK, 2 * h), lambda i, s: (i, 0, 0)),
        ),
        out_shape=jax.ShapeDtypeStruct((ctx * CAP, BLK, 2 * h), BF16),
        compiler_params=PARAMS,
    )(sources, keys, values)
    kv_out, pair[1], kv_before, kv_after, kv_glob = lax.optimization_barrier((kv_out, pair[1], kv_before, kv_after, kv_glob))
    kv_in = lax.all_to_all(kv_out.reshape(ctx, CAP, BLK, 2 * h), "ctx", 0, 0, tiled=True)
    kv_in = kv_in.reshape(ctx * CAP, BLK, 2 * h)

    all_tiles, all_heads = list(pair), [my_head, my_head ^ 1]
    for far in range(2, heads, 2):
        there = [(i, (i + far) % heads) for i in range(heads)]
        all_tiles += [lax.ppermute(t, "head", there) for t in pair]
        source = (my_head - far) % heads
        all_heads += [source, source ^ 1]

    every = jnp.arange(D, dtype=jnp.int32)
    table_new = proj_table(step_codes[1], rank_ids, every)
    table_old = proj_table(step_codes[0], rank_ids, every)
    share = momentum.shape[1]
    carried = pl.pallas_call(
        carry,
        in_specs=[VMEM] * 3,
        out_specs=VMEM,
        out_shape=jax.ShapeDtypeStruct((8, RANK), F32),
        compiler_params=PARAMS,
    )(jnp.pad(momentum[0], ((0, 8 - share), (0, 0))), table_old, table_new)

    edges = jnp.stack([my_ctx == 0, my_ctx == ctx - 1]).astype(jnp.int32)
    unroll = 2
    wide = pl.BlockSpec((unroll * BLK, GROUP * h), lambda i: (i, 0))
    dq, grad = pl.pallas_call(
        attend,
        grid=(blocks // unroll,),
        in_specs=[SMEM] * 3 + [wide] * 2 + [VMEM] * (6 + heads) + [ANY] * 2,
        out_specs=[wide, VMEM],
        out_shape=[
            jax.ShapeDtypeStruct((tokens, GROUP * h), BF16),
            jax.ShapeDtypeStruct((ctx, 2 * share, 128), F32),
        ],
        scratch_shapes=[
            pltpu.VMEM((tokens + 2 * BLK, h), BF16),
            pltpu.VMEM((tokens + 2 * BLK, h), BF16),
            pltpu.VMEM((tokens + 2 * BLK, 2 * h), F32),
            pltpu.VMEM((GLOB * BLK, 2 * h), F32),
            pltpu.VMEM((PARTS, places, ROWS, 2 * h), BF16),
            pltpu.VMEM((2, 2 * h, 128), F32),
        ],
        compiler_params=LARGE,
    )(
        arrival, edges, jnp.stack(all_heads), queries, d_attn, keys, values, kv_before, kv_after, kv_glob, kv_in,
        *all_tiles, table_new, carried,
    )
    grad = lax.all_to_all(grad, "ctx", 0, 0, tiled=True)
    new_momentum, weight_step = pl.pallas_call(
        functools.partial(finish, 1.0 / math.sqrt(tokens * ctx)),
        in_specs=[VMEM] * 3,
        out_specs=[VMEM] * 2,
        out_shape=[
            jax.ShapeDtypeStruct((share, RANK), F32),
            jax.ShapeDtypeStruct((share, D), F32),
        ],
        compiler_params=PARAMS,
    )(grad, carried, table_new)
    return dq, new_momentum[None], weight_step[None]


def solution(mesh):
    in_specs = (
        P("ctx", "head"),
        P("ctx", "head"),
        P("ctx", "head"),
        P("ctx", "head"),
        P("ctx", "head"),
        P(),
        P(),
        P(),
        P("head", "ctx", None),
    )
    out_specs = (P("ctx", "head"), P("head", "ctx", None), P("head", "ctx", None))
    return jax.shard_map(local, mesh=mesh, in_specs=in_specs, out_specs=out_specs, check_vma=False)
```

```python
import functools
import math

import jax
import jax.numpy as jnp
from jax import lax
from jax.experimental import pallas as pl
from jax.experimental.pallas import tpu as pltpu
from jax.sharding import PartitionSpec as P

D = 4096
HEAD_SIZE = 128
GROUP = 4
BLK = 64
RAND = 3
GLOB = 2
RANK = 256
CAP = 2
ROWS = 16
PARTS = BLK // ROWS
F32 = jnp.float32
BF16 = jnp.bfloat16
VMEM = pl.BlockSpec(memory_space=pltpu.VMEM)
ANY = pl.BlockSpec(memory_space=pl.ANY)
SMEM = pl.BlockSpec(memory_space=pltpu.SMEM)
PARAMS = pltpu.CompilerParams(vmem_limit_bytes=16 * 1024 * 1024)
LARGE = pltpu.CompilerParams(vmem_limit_bytes=30 * 1024 * 1024)


def proj_table(code_value, rank_ids, feature_ids):
    row_ids = rank_ids[:, None]
    col_ids = feature_ids[None, :]
    section_one = (row_ids * 31337 + col_ids * 7919 + code_value * 10007) % 65521
    section_two = (section_one * 181 + section_one % 251 * 4093 + col_ids) % 65521
    section_three = (section_two * (section_two % 127 + 1) + row_ids * 17) % 65521
    unit_value = (section_three.astype(jnp.float32) + 0.5) / 65521.0 - 0.5
    return (unit_value * math.sqrt(12.0 / D)).astype(jnp.bfloat16)


def dot(a, b, da, db):
    return lax.dot_general(a, b, (((da,), (db,)), ((), ())), preferred_element_type=F32)


def split3(x):
    high = x.astype(BF16)
    rest = x - high.astype(F32)
    mid = rest.astype(BF16)
    return high, mid, (rest - mid.astype(F32)).astype(BF16)


def pack_kv(src_ref, k_ref, v_ref, out_ref):
    here = out_ref.shape[0]
    first = pl.program_id(0) * here
    for i in range(here):
        rows = pl.ds(pl.multiple_of(src_ref[first + i] * BLK, BLK), BLK)
        out_ref[i, :, :HEAD_SIZE] = k_ref[rows, :]
        out_ref[i, :, HEAD_SIZE:] = v_ref[rows, :]


def project(x_ref, t_ref, out_ref):
    blocks = out_ref.shape[1]
    y = dot(x_ref[...], t_ref[...], 1, 1).astype(out_ref.dtype)
    for b in range(blocks):
        for part in range(PARTS):
            row = b * BLK + part * ROWS
            for half in range(2):
                out_ref[half * PARTS + part, b] = y[row : row + ROWS, half * 128 : half * 128 + 128]


def sum_pack(src_ref, gid_ref, x_ref, own_ref, out_ref, acc):
    own = x_ref[0].astype(F32)
    for i in range(1, x_ref.shape[0]):
        own = own + x_ref[i].astype(F32)
    acc[...] = own.astype(BF16)
    own_ref[...] = acc[...]
    for i in range(out_ref.shape[0]):
        for c in range(CAP):
            out_ref[i, c] = acc[src_ref[i * CAP + c]]
        for g in range(GLOB):
            out_ref[i, CAP + g] = acc[gid_ref[g]]


def collect(arrival_ref, owner_ref, own_ref, before_ref, after_ref, recv_ref, out_ref):
    blocks = own_ref.shape[0]
    tiles = [before_ref[...]] + [own_ref[b] for b in range(blocks)] + [after_ref[...]]
    tiles += [recv_ref[owner_ref[g] * (CAP + GLOB) + CAP + g] for g in range(GLOB)]
    tiles += [recv_ref[arrival_ref[n] // CAP * (CAP + GLOB) + arrival_ref[n] % CAP] for n in range(blocks * RAND)]
    for n, tile in enumerate(tiles):
        out_ref[n] = tile


def attend(
    arrival_ref, edge_ref, from_ref, q_ref, g_ref, k_ref, v_ref, before_ref, after_ref, glob_ref, recv_ref, *refs
):
    dq_ref, out_ref, kwin, vwin, wacc, gacc, kg_ref, total = refs[-8:]
    tile_refs = refs[:-10]
    step, steps = pl.program_id(0), pl.num_programs(0)
    tokens = k_ref.shape[0]
    blocks = tokens // BLK
    unroll = q_ref.shape[0] // BLK
    scaling = 1.0 / math.sqrt(HEAD_SIZE)
    h = HEAD_SIZE

    @pl.when(step == 0)
    def _():
        for win, ref, low in ((kwin, k_ref, 0), (vwin, v_ref, h)):
            win[:BLK] = before_ref[:, low : low + h]
            win[BLK : BLK + tokens] = ref[...]
            win[BLK + tokens :] = after_ref[:, low : low + h]
        wacc[...] = jnp.zeros_like(wacc)
        gacc[...] = jnp.zeros_like(gacc)

    for u in range(unroll):
        b = step * unroll + u
        rows = pl.ds(pl.multiple_of(b * BLK, BLK), 3 * BLK)
        picks = [arrival_ref[b * RAND + r] for r in range(RAND)]
        k_all = jnp.concatenate([kwin[rows, :]] + [recv_ref[p, :, :h] for p in picks] + [glob_ref[:, :h]], axis=0)
        v_all = jnp.concatenate([vwin[rows, :]] + [recv_ref[p, :, h:] for p in picks] + [glob_ref[:, h:]], axis=0)
        here = slice(u * BLK, (u + 1) * BLK)
        q = jnp.concatenate([q_ref[here, j * h : (j + 1) * h] for j in range(GROUP)], axis=0)
        g = jnp.concatenate([g_ref[here, j * h : (j + 1) * h] for j in range(GROUP)], axis=0)
        s = dot(k_all, q, 1, 1) * (scaling * math.log2(math.e))
        left = jnp.where(b == 0, edge_ref[0], 0).astype(F32) * -1e30
        right = jnp.where(b == blocks - 1, edge_ref[1], 0).astype(F32) * -1e30
        s = jnp.concatenate(
            [s[:BLK] + left, s[BLK : 2 * BLK], s[2 * BLK : 3 * BLK] + right, s[3 * BLK :]], axis=0
        )
        e = jnp.exp2(s - jnp.max(s, axis=0, keepdims=True))
        w = e * (1.0 / jnp.sum(e, axis=0, keepdims=True))
        w_bf = w.astype(BF16)
        dw = dot(v_all, g, 1, 1)
        delta = jnp.sum(w_bf.astype(F32) * dw, axis=0, keepdims=True)
        ds = (w * (dw - delta)).astype(BF16)
        dq = jnp.transpose(dot(k_all, ds, 0, 0) * scaling).astype(BF16)
        for j in range(GROUP):
            dq_ref[here, j * h : (j + 1) * h] = dq[j * BLK : (j + 1) * BLK]
        kg = dot(ds, q, 1, 0) * scaling
        vg = dot(w_bf, g, 1, 0)
        wacc[rows, :h] += kg[: 3 * BLK]
        wacc[rows, h:] += vg[: 3 * BLK]
        gacc[:, :h] += kg[(3 + RAND) * BLK :]
        gacc[:, h:] += vg[(3 + RAND) * BLK :]
        for r in range(RAND):
            for part in range(PARTS):
                low = (3 + r) * BLK + part * ROWS
                place = blocks + 2 + GLOB + b * RAND + r
                kg_ref[part, place, :, :h] = kg[low : low + ROWS].astype(BF16)
                kg_ref[part, place, :, h:] = vg[low : low + ROWS].astype(BF16)

    @pl.when(step == steps - 1)
    def _():
        for acc, first, count in ((wacc, 0, blocks + 2), (gacc, blocks + 2, GLOB)):
            for n in range(count):
                for part in range(PARTS):
                    low = n * BLK + part * ROWS
                    kg_ref[part, first + n] = acc[low : low + ROWS, :].astype(BF16)
        total[...] = jnp.zeros_like(total)
        many = kg_ref.shape[1] * ROWS
        for i, ref in enumerate(tile_refs):
            head = from_ref[i]
            kg = kg_ref[head % PARTS].reshape(many, 2 * h)
            total[head // PARTS] += dot(kg, ref[...].reshape(many, 128), 0, 0)
        rows = total.shape[1] // out_ref.shape[0]
        for d in range(out_ref.shape[0]):
            for half in range(2):
                out_ref[d, half * rows : (half + 1) * rows] = total[half, d * rows : (d + 1) * rows]


def carry(m_ref, old_ref, new_ref, out_ref):
    rows = m_ref.shape[0]
    x = dot(jnp.concatenate(split3(m_ref[...]), axis=0), old_ref[...], 1, 0)
    x = x[:rows] + x[rows : 2 * rows] + x[2 * rows :]
    y = dot(jnp.concatenate(split3(x), axis=0), new_ref[...], 1, 1)
    out_ref[...] = 0.9 * (y[:rows] + y[rows : 2 * rows] + y[2 * rows :])


def finish(scale, recv_ref, carried_ref, new_ref, mom_ref, step_ref):
    rows = mom_ref.shape[0]
    grad = jnp.sum(recv_ref[...], axis=0) * scale
    total = carried_ref[:rows] + jnp.concatenate([grad[:rows], grad[rows:]], axis=1)
    mom_ref[...] = total
    padded = jnp.concatenate([total, jnp.zeros((8 - rows, RANK), F32)], axis=0)
    y = dot(jnp.concatenate(split3(padded), axis=0), new_ref[...], 1, 0)
    step_ref[...] = (y[:8] + y[8:16] + y[16:])[:rows]


def local(queries, keys, values, d_attn, inputs, random_ids, global_ids, step_codes, momentum):
    tokens = queries.shape[0]
    blocks = tokens // BLK
    ctx, heads = lax.axis_size("ctx"), lax.axis_size("head")
    my_ctx, my_head = lax.axis_index("ctx"), lax.axis_index("head")
    requests = blocks * RAND
    places = blocks + 2 + GLOB + requests
    h = HEAD_SIZE
    up = [(i, i + 1) for i in range(ctx - 1)]
    down = [(i + 1, i) for i in range(ctx - 1)]

    ids = random_ids.reshape(ctx, requests)
    owners, inner = ids // blocks, ids % blocks
    order = jnp.arange(requests, dtype=jnp.int32)
    tagged = order[None, :] * blocks + inner
    mine = owners == my_ctx
    first = jnp.min(jnp.where(mine, tagged, requests * blocks), axis=1) % blocks
    last = jnp.max(jnp.where(mine, tagged, 0), axis=1) % blocks
    sources = jnp.stack([first, last], axis=1).reshape(-1)
    my_owners = lax.dynamic_index_in_dim(owners, my_ctx, 0, keepdims=False)
    earlier = (my_owners[:, None] == my_owners[None, :]) & (order[None, :] < order[:, None])
    arrival = my_owners * CAP + jnp.any(earlier, axis=1).astype(jnp.int32)
    global_owner, global_inner = global_ids // blocks, global_ids % blocks

    feature_ids = my_head * inputs.shape[1] + jnp.arange(inputs.shape[1], dtype=jnp.int32)
    rank_ids = jnp.arange(RANK, dtype=jnp.int32)
    table_part = proj_table(step_codes[1], rank_ids, feature_ids)
    terms = pl.pallas_call(
        project,
        in_specs=[VMEM] * 2,
        out_specs=VMEM,
        out_shape=jax.ShapeDtypeStruct((heads, blocks, ROWS, 128), BF16),
        compiler_params=PARAMS,
    )(inputs, table_part)
    terms = lax.all_to_all(terms, "head", 0, 0, tiled=True)
    own, p_out = pl.pallas_call(
        sum_pack,
        in_specs=[SMEM, SMEM, VMEM],
        out_specs=[VMEM] * 2,
        out_shape=[
            jax.ShapeDtypeStruct((blocks, ROWS, 128), BF16),
            jax.ShapeDtypeStruct((ctx, CAP + GLOB, ROWS, 128), BF16),
        ],
        scratch_shapes=[pltpu.VMEM((blocks, ROWS, 128), BF16)],
        compiler_params=PARAMS,
    )(sources, global_inner, terms)

    kv_before = lax.ppermute(jnp.concatenate([keys[-BLK:], values[-BLK:]], axis=1), "ctx", up)
    kv_after = lax.ppermute(jnp.concatenate([keys[:BLK], values[:BLK]], axis=1), "ctx", down)
    kv_glob = []
    for g in range(GLOB):
        row = global_inner[g] * BLK
        kv_glob.append(jnp.concatenate([lax.dynamic_slice_in_dim(x, row, BLK, 0) for x in (keys, values)], axis=1))
    kv_glob = jnp.stack(kv_glob)
    apart = my_ctx ^ global_owner
    bit = 1
    while bit < ctx:
        other = lax.ppermute(kv_glob, "ctx", [(i, i ^ bit) for i in range(ctx)])
        kv_glob = jnp.where(((apart & bit) != 0)[:, None, None], other, kv_glob)
        bit *= 2
    kv_glob = kv_glob.reshape(GLOB * BLK, 2 * h)

    p_out, kv_glob, kv_before, kv_after = lax.optimization_barrier((p_out, kv_glob, kv_before, kv_after))
    p_in = lax.all_to_all(p_out, "ctx", 0, 0, tiled=True)
    p_before = lax.ppermute(own[-1], "ctx", up)
    p_after = lax.ppermute(own[0], "ctx", down)
    tiles = pl.pallas_call(
        collect,
        in_specs=[SMEM, SMEM] + [VMEM] * 4,
        out_specs=VMEM,
        out_shape=jax.ShapeDtypeStruct((places, ROWS, 128), BF16),
        compiler_params=PARAMS,
    )(arrival, global_owner, own, p_before, p_after, p_in.reshape(ctx * (CAP + GLOB), ROWS, 128))
    pair = [tiles, lax.ppermute(tiles, "head", [(i, i ^ 1) for i in range(heads)])]
    chunk = 16
    kv_out = pl.pallas_call(
        pack_kv,
        grid_spec=pltpu.PrefetchScalarGridSpec(
            num_scalar_prefetch=1,
            grid=(ctx * CAP // chunk,),
            in_specs=[VMEM, VMEM],
            out_specs=pl.BlockSpec((chunk, BLK, 2 * h), lambda i, s: (i, 0, 0)),
        ),
        out_shape=pltpu.HBM((ctx * CAP, BLK, 2 * h), BF16),
        compiler_params=PARAMS,
    )(sources, keys, values)
    kv_out, pair[1], kv_before, kv_after, kv_glob = lax.optimization_barrier((kv_out, pair[1], kv_before, kv_after, kv_glob))
    kv_in = lax.all_to_all(kv_out.reshape(ctx, CAP, BLK, 2 * h), "ctx", 0, 0, tiled=True)
    kv_in = kv_in.reshape(ctx * CAP, BLK, 2 * h)

    all_tiles, all_heads = list(pair), [my_head, my_head ^ 1]
    for far in range(2, heads, 2):
        there = [(i, (i + far) % heads) for i in range(heads)]
        all_tiles += [lax.ppermute(t, "head", there) for t in pair]
        source = (my_head - far) % heads
        all_heads += [source, source ^ 1]

    every = jnp.arange(D, dtype=jnp.int32)
    table_new = proj_table(step_codes[1], rank_ids, every)
    table_old = proj_table(step_codes[0], rank_ids, every)
    share = momentum.shape[1]
    carried = pl.pallas_call(
        carry,
        in_specs=[VMEM] * 3,
        out_specs=VMEM,
        out_shape=jax.ShapeDtypeStruct((8, RANK), F32),
        compiler_params=PARAMS,
    )(jnp.pad(momentum[0], ((0, 8 - share), (0, 0))), table_old, table_new)

    edges = jnp.stack([my_ctx == 0, my_ctx == ctx - 1]).astype(jnp.int32)
    unroll = 2
    wide = pl.BlockSpec((unroll * BLK, GROUP * h), lambda i: (i, 0))
    dq, grad = pl.pallas_call(
        attend,
        grid=(blocks // unroll,),
        in_specs=[SMEM] * 3 + [wide] * 2 + [VMEM] * (6 + heads) + [ANY] * 2,
        out_specs=[wide, VMEM],
        out_shape=[
            jax.ShapeDtypeStruct((tokens, GROUP * h), BF16),
            pltpu.HBM((ctx, 2 * share, 128), F32),
        ],
        scratch_shapes=[
            pltpu.VMEM((tokens + 2 * BLK, h), BF16),
            pltpu.VMEM((tokens + 2 * BLK, h), BF16),
            pltpu.VMEM((tokens + 2 * BLK, 2 * h), F32),
            pltpu.VMEM((GLOB * BLK, 2 * h), F32),
            pltpu.VMEM((PARTS, places, ROWS, 2 * h), BF16),
            pltpu.VMEM((2, 2 * h, 128), F32),
        ],
        compiler_params=LARGE,
    )(
        arrival, edges, jnp.stack(all_heads), queries, d_attn, keys, values, kv_before, kv_after, kv_glob, kv_in,
        *all_tiles, table_new, carried,
    )
    grad = lax.all_to_all(grad, "ctx", 0, 0, tiled=True)
    new_momentum, weight_step = pl.pallas_call(
        functools.partial(finish, 1.0 / math.sqrt(tokens * ctx)),
        in_specs=[VMEM] * 3,
        out_specs=[VMEM] * 2,
        out_shape=[
            jax.ShapeDtypeStruct((share, RANK), F32),
            jax.ShapeDtypeStruct((share, D), F32),
        ],
        compiler_params=PARAMS,
    )(grad, carried, table_new)
    return dq, new_momentum[None], weight_step[None]


def solution(mesh):
    in_specs = (
        P("ctx", "head"),
        P("ctx", "head"),
        P("ctx", "head"),
        P("ctx", "head"),
        P("ctx", "head"),
        P(),
        P(),
        P(),
        P("head", "ctx", None),
    )
    out_specs = (P("ctx", "head"), P("head", "ctx", None), P("head", "ctx", None))
    return jax.shard_map(local, mesh=mesh, in_specs=in_specs, out_specs=out_specs, check_vma=False)
```

```python
import functools
import math

import jax
import jax.numpy as jnp
from jax import lax
from jax.experimental import pallas as pl
from jax.experimental.pallas import tpu as pltpu
from jax.sharding import PartitionSpec as P

D = 4096
HEAD_SIZE = 128
GROUP = 4
BLK = 64
RAND = 3
GLOB = 2
RANK = 256
CAP = 2
ROWS = 16
PARTS = BLK // ROWS
F32 = jnp.float32
BF16 = jnp.bfloat16
VMEM = pl.BlockSpec(memory_space=pltpu.VMEM)
ANY = pl.BlockSpec(memory_space=pl.ANY)
SMEM = pl.BlockSpec(memory_space=pltpu.SMEM)
PARAMS = pltpu.CompilerParams(vmem_limit_bytes=16 * 1024 * 1024)
LARGE = pltpu.CompilerParams(vmem_limit_bytes=30 * 1024 * 1024)


def proj_table(code_value, rank_ids, feature_ids):
    row_ids = rank_ids[:, None]
    col_ids = feature_ids[None, :]
    section_one = (row_ids * 31337 + col_ids * 7919 + code_value * 10007) % 65521
    section_two = (section_one * 181 + section_one % 251 * 4093 + col_ids) % 65521
    section_three = (section_two * (section_two % 127 + 1) + row_ids * 17) % 65521
    unit_value = (section_three.astype(jnp.float32) + 0.5) / 65521.0 - 0.5
    return (unit_value * math.sqrt(12.0 / D)).astype(jnp.bfloat16)


def dot(a, b, da, db):
    return lax.dot_general(a, b, (((da,), (db,)), ((), ())), preferred_element_type=F32)


def split3(x):
    high = x.astype(BF16)
    rest = x - high.astype(F32)
    mid = rest.astype(BF16)
    return high, mid, (rest - mid.astype(F32)).astype(BF16)


def pack_kv(src_ref, owner_ref, k_ref, v_ref, tile_ref, out_ref):
    here = out_ref.shape[0]
    first = pl.program_id(0) * here
    for i in range(here):
        for c in range(CAP):
            rows = pl.ds(pl.multiple_of(src_ref[(first + i) * CAP + c] * BLK, BLK), BLK)
            out_ref[i, 2 * c * BLK : (2 * c + 1) * BLK] = k_ref[rows, :]
            out_ref[i, (2 * c + 1) * BLK : (2 * c + 2) * BLK] = v_ref[rows, :]
        out_ref[i, 2 * CAP * BLK :] = tile_ref[owner_ref[0], CAP + GLOB]


def project(x_ref, t_ref, out_ref):
    blocks = out_ref.shape[1]
    y = dot(x_ref[...], t_ref[...], 1, 1).astype(out_ref.dtype)
    for b in range(blocks):
        for part in range(PARTS):
            row = b * BLK + part * ROWS
            for half in range(2):
                out_ref[half * PARTS + part, b] = y[row : row + ROWS, half * 128 : half * 128 + 128]


def sum_pack(src_ref, gid_ref, x_ref, k_ref, v_ref, own_ref, out_ref, acc):
    own = x_ref[0].astype(F32)
    for i in range(1, x_ref.shape[0]):
        own = own + x_ref[i].astype(F32)
    acc[...] = own.astype(BF16)
    own_ref[...] = acc[...]
    for i in range(out_ref.shape[0]):
        for c in range(CAP):
            out_ref[i, c] = acc[src_ref[i * CAP + c]]
        for g in range(GLOB):
            out_ref[i, CAP + g] = acc[gid_ref[g]]
        if i < 2 * GLOB * PARTS:
            row = gid_ref[i // (2 * PARTS)] * BLK + i % PARTS * ROWS
            ref = (k_ref, v_ref)[i // PARTS % 2]
            out_ref[i, CAP + GLOB] = ref[pl.ds(pl.multiple_of(row, ROWS), ROWS), :]
        else:
            out_ref[i, CAP + GLOB] = jnp.zeros((ROWS, 128), BF16)


def collect(arrival_ref, owner_ref, own_ref, before_ref, after_ref, recv_ref, out_ref):
    blocks = own_ref.shape[0]
    tiles = [before_ref[...]] + [own_ref[b] for b in range(blocks)] + [after_ref[...]]
    tiles += [recv_ref[owner_ref[g], CAP + g] for g in range(GLOB)]
    tiles += [recv_ref[arrival_ref[n] // CAP, arrival_ref[n] % CAP] for n in range(blocks * RAND)]
    for n, tile in enumerate(tiles):
        out_ref[n] = tile


def attend(
    arrival_ref, edge_ref, from_ref, q_ref, g_ref, k_ref, v_ref, before_ref, after_ref, recv_ref, *refs
):
    dq_ref, out_ref, kwin, vwin, kglob, vglob, wacc, gacc, kg_ref, total = refs[-10:]
    tile_refs = refs[:-12]
    step, steps = pl.program_id(0), pl.num_programs(0)
    tokens = k_ref.shape[0]
    blocks = tokens // BLK
    unroll = q_ref.shape[0] // BLK
    scaling = 1.0 / math.sqrt(HEAD_SIZE)
    h = HEAD_SIZE

    @pl.when(step == 0)
    def _():
        for win, ref, low in ((kwin, k_ref, 0), (vwin, v_ref, h)):
            win[:BLK] = before_ref[:, low : low + h]
            win[BLK : BLK + tokens] = ref[...]
            win[BLK + tokens :] = after_ref[:, low : low + h]
        for kind, ref in enumerate((kglob, vglob)):
            for g in range(GLOB):
                for part in range(PARTS):
                    tile = recv_ref[(2 * g + kind) * PARTS + part, 2 * CAP * BLK :]
                    ref[g * BLK + part * ROWS : g * BLK + (part + 1) * ROWS] = tile
        wacc[...] = jnp.zeros_like(wacc)
        gacc[...] = jnp.zeros_like(gacc)

    for u in range(unroll):
        b = step * unroll + u
        rows = pl.ds(pl.multiple_of(b * BLK, BLK), 3 * BLK)
        picks = [arrival_ref[b * RAND + r] for r in range(RAND)]
        at = [(p // CAP, pl.multiple_of(p % CAP * (2 * BLK), BLK)) for p in picks]
        k_all = jnp.concatenate([kwin[rows, :]] + [recv_ref[o, pl.ds(i, BLK), :] for o, i in at] + [kglob[...]], axis=0)
        v_all = jnp.concatenate(
            [vwin[rows, :]] + [recv_ref[o, pl.ds(i + BLK, BLK), :] for o, i in at] + [vglob[...]], axis=0
        )
        here = slice(u * BLK, (u + 1) * BLK)
        q = jnp.concatenate([q_ref[here, j * h : (j + 1) * h] for j in range(GROUP)], axis=0)
        g = jnp.concatenate([g_ref[here, j * h : (j + 1) * h] for j in range(GROUP)], axis=0)
        s = dot(k_all, q, 1, 1) * (scaling * math.log2(math.e))
        left = jnp.where(b == 0, edge_ref[0], 0).astype(F32) * -1e30
        right = jnp.where(b == blocks - 1, edge_ref[1], 0).astype(F32) * -1e30
        s = jnp.concatenate(
            [s[:BLK] + left, s[BLK : 2 * BLK], s[2 * BLK : 3 * BLK] + right, s[3 * BLK :]], axis=0
        )
        e = jnp.exp2(s - jnp.max(s, axis=0, keepdims=True))
        w = e * (1.0 / jnp.sum(e, axis=0, keepdims=True))
        w_bf = w.astype(BF16)
        dw = dot(v_all, g, 1, 1)
        delta = jnp.sum(w_bf.astype(F32) * dw, axis=0, keepdims=True)
        ds = (w * (dw - delta)).astype(BF16)
        dq = jnp.transpose(dot(k_all, ds, 0, 0) * scaling).astype(BF16)
        for j in range(GROUP):
            dq_ref[here, j * h : (j + 1) * h] = dq[j * BLK : (j + 1) * BLK]
        kg = dot(ds, q, 1, 0) * scaling
        vg = dot(w_bf, g, 1, 0)
        wacc[rows, :h] += kg[: 3 * BLK]
        wacc[rows, h:] += vg[: 3 * BLK]
        gacc[:, :h] += kg[(3 + RAND) * BLK :]
        gacc[:, h:] += vg[(3 + RAND) * BLK :]
        for r in range(RAND):
            for part in range(PARTS):
                low = (3 + r) * BLK + part * ROWS
                place = blocks + 2 + GLOB + b * RAND + r
                kg_ref[part, place, :, :h] = kg[low : low + ROWS].astype(BF16)
                kg_ref[part, place, :, h:] = vg[low : low + ROWS].astype(BF16)

    @pl.when(step == steps - 1)
    def _():
        for acc, first, count in ((wacc, 0, blocks + 2), (gacc, blocks + 2, GLOB)):
            for n in range(count):
                for part in range(PARTS):
                    low = n * BLK + part * ROWS
                    kg_ref[part, first + n] = acc[low : low + ROWS, :].astype(BF16)
        total[...] = jnp.zeros_like(total)
        many = kg_ref.shape[1] * ROWS
        for i, ref in enumerate(tile_refs):
            head = from_ref[i]
            kg = kg_ref[head % PARTS].reshape(many, 2 * h)
            total[head // PARTS] += dot(kg, ref[...].reshape(many, 128), 0, 0)
        rows = total.shape[1] // out_ref.shape[0]
        for d in range(out_ref.shape[0]):
            for half in range(2):
                out_ref[d, half * rows : (half + 1) * rows] = total[half, d * rows : (d + 1) * rows]


def carry(m_ref, old_ref, new_ref, out_ref):
    rows = m_ref.shape[0]
    x = dot(jnp.concatenate(split3(m_ref[...]), axis=0), old_ref[...], 1, 0)
    x = x[:rows] + x[rows : 2 * rows] + x[2 * rows :]
    y = dot(jnp.concatenate(split3(x), axis=0), new_ref[...], 1, 1)
    out_ref[...] = 0.9 * (y[:rows] + y[rows : 2 * rows] + y[2 * rows :])


def finish(scale, recv_ref, carried_ref, new_ref, mom_ref, step_ref):
    rows = mom_ref.shape[0]
    grad = jnp.sum(recv_ref[...], axis=0) * scale
    total = carried_ref[:rows] + jnp.concatenate([grad[:rows], grad[rows:]], axis=1)
    mom_ref[...] = total
    padded = jnp.concatenate([total, jnp.zeros((8 - rows, RANK), F32)], axis=0)
    y = dot(jnp.concatenate(split3(padded), axis=0), new_ref[...], 1, 0)
    step_ref[...] = (y[:8] + y[8:16] + y[16:])[:rows]


def local(queries, keys, values, d_attn, inputs, random_ids, global_ids, step_codes, momentum):
    tokens = queries.shape[0]
    blocks = tokens // BLK
    ctx, heads = lax.axis_size("ctx"), lax.axis_size("head")
    my_ctx, my_head = lax.axis_index("ctx"), lax.axis_index("head")
    requests = blocks * RAND
    places = blocks + 2 + GLOB + requests
    h = HEAD_SIZE
    up = [(i, i + 1) for i in range(ctx - 1)]
    down = [(i + 1, i) for i in range(ctx - 1)]

    ids = random_ids.reshape(ctx, requests)
    owners, inner = ids // blocks, ids % blocks
    order = jnp.arange(requests, dtype=jnp.int32)
    tagged = order[None, :] * blocks + inner
    mine = owners == my_ctx
    first = jnp.min(jnp.where(mine, tagged, requests * blocks), axis=1) % blocks
    last = jnp.max(jnp.where(mine, tagged, 0), axis=1) % blocks
    sources = jnp.stack([first, last], axis=1).reshape(-1)
    my_owners = lax.dynamic_index_in_dim(owners, my_ctx, 0, keepdims=False)
    earlier = (my_owners[:, None] == my_owners[None, :]) & (order[None, :] < order[:, None])
    arrival = my_owners * CAP + jnp.any(earlier, axis=1).astype(jnp.int32)
    global_owner, global_inner = global_ids // blocks, global_ids % blocks

    feature_ids = my_head * inputs.shape[1] + jnp.arange(inputs.shape[1], dtype=jnp.int32)
    rank_ids = jnp.arange(RANK, dtype=jnp.int32)
    table_part = proj_table(step_codes[1], rank_ids, feature_ids)
    terms = pl.pallas_call(
        project,
        in_specs=[VMEM] * 2,
        out_specs=VMEM,
        out_shape=jax.ShapeDtypeStruct((heads, blocks, ROWS, 128), BF16),
        compiler_params=PARAMS,
    )(inputs, table_part)
    terms = lax.all_to_all(terms, "head", 0, 0, tiled=True)
    own, p_out = pl.pallas_call(
        sum_pack,
        in_specs=[SMEM, SMEM] + [VMEM] * 3,
        out_specs=[VMEM] * 2,
        out_shape=[
            jax.ShapeDtypeStruct((blocks, ROWS, 128), BF16),
            jax.ShapeDtypeStruct((ctx, CAP + GLOB + 1, ROWS, 128), BF16),
        ],
        scratch_shapes=[pltpu.VMEM((blocks, ROWS, 128), BF16)],
        compiler_params=PARAMS,
    )(sources, global_inner, terms, keys, values)

    kv_before = lax.ppermute(jnp.concatenate([keys[-BLK:], values[-BLK:]], axis=1), "ctx", up)
    kv_after = lax.ppermute(jnp.concatenate([keys[:BLK], values[:BLK]], axis=1), "ctx", down)
    p_in = lax.all_to_all(p_out, "ctx", 0, 0, tiled=True)
    p_before = lax.ppermute(own[-1], "ctx", up)
    p_after = lax.ppermute(own[0], "ctx", down)

    chunk = 8
    tile_owner = global_owner[jnp.minimum(my_ctx // (2 * PARTS), GLOB - 1)]
    span = 2 * CAP * BLK + ROWS
    kv_out = pl.pallas_call(
        pack_kv,
        grid_spec=pltpu.PrefetchScalarGridSpec(
            num_scalar_prefetch=2,
            grid=(ctx // chunk,),
            in_specs=[VMEM] * 3,
            out_specs=pl.BlockSpec((chunk, span, h), lambda i, s, o: (i, 0, 0)),
        ),
        out_shape=pltpu.HBM((ctx, span, h), BF16),
        compiler_params=PARAMS,
    )(sources, tile_owner.reshape(1), keys, values, p_in)
    kv_out, kv_before, kv_after, p_before, p_after = lax.optimization_barrier(
        (kv_out, kv_before, kv_after, p_before, p_after)
    )
    kv_in = lax.all_to_all(kv_out, "ctx", 0, 0, tiled=True)

    tiles = pl.pallas_call(
        collect,
        in_specs=[SMEM, SMEM] + [VMEM] * 4,
        out_specs=VMEM,
        out_shape=jax.ShapeDtypeStruct((places, ROWS, 128), BF16),
        compiler_params=PARAMS,
    )(arrival, global_owner, own, p_before, p_after, p_in)
    pair = [tiles, lax.ppermute(tiles, "head", [(i, i ^ 1) for i in range(heads)])]
    every = jnp.arange(D, dtype=jnp.int32)
    table_new = proj_table(step_codes[1], rank_ids, every)
    table_old = proj_table(step_codes[0], rank_ids, every)
    share = momentum.shape[1]
    carried = pl.pallas_call(
        carry,
        in_specs=[VMEM] * 3,
        out_specs=VMEM,
        out_shape=jax.ShapeDtypeStruct((8, RANK), F32),
        compiler_params=PARAMS,
    )(jnp.pad(momentum[0], ((0, 8 - share), (0, 0))), table_old, table_new)

    pair[1], carried = lax.optimization_barrier((pair[1], carried))
    all_tiles, all_heads = list(pair), [my_head, my_head ^ 1]
    for far in range(2, heads, 2):
        there = [(i, (i + far) % heads) for i in range(heads)]
        all_tiles += [lax.ppermute(t, "head", there) for t in pair]
        source = (my_head - far) % heads
        all_heads += [source, source ^ 1]

    edges = jnp.stack([my_ctx == 0, my_ctx == ctx - 1]).astype(jnp.int32)
    unroll = 2
    wide = pl.BlockSpec((unroll * BLK, GROUP * h), lambda i: (i, 0))
    dq, grad = pl.pallas_call(
        attend,
        grid=(blocks // unroll,),
        in_specs=[SMEM] * 3 + [wide] * 2 + [VMEM] * (5 + heads) + [ANY] * 2,
        out_specs=[wide, VMEM],
        out_shape=[
            jax.ShapeDtypeStruct((tokens, GROUP * h), BF16),
            pltpu.HBM((ctx, 2 * share, 128), F32),
        ],
        scratch_shapes=[
            pltpu.VMEM((tokens + 2 * BLK, h), BF16),
            pltpu.VMEM((tokens + 2 * BLK, h), BF16),
            pltpu.VMEM((GLOB * BLK, h), BF16),
            pltpu.VMEM((GLOB * BLK, h), BF16),
            pltpu.VMEM((tokens + 2 * BLK, 2 * h), F32),
            pltpu.VMEM((GLOB * BLK, 2 * h), F32),
            pltpu.VMEM((PARTS, places, ROWS, 2 * h), BF16),
            pltpu.VMEM((2, 2 * h, 128), F32),
        ],
        compiler_params=LARGE,
    )(
        arrival, edges, jnp.stack(all_heads), queries, d_attn, keys, values, kv_before, kv_after, kv_in,
        *all_tiles, table_new, carried,
    )
    grad = lax.all_to_all(grad, "ctx", 0, 0, tiled=True)
    new_momentum, weight_step = pl.pallas_call(
        functools.partial(finish, 1.0 / math.sqrt(tokens * ctx)),
        in_specs=[VMEM] * 3,
        out_specs=[VMEM] * 2,
        out_shape=[
            jax.ShapeDtypeStruct((share, RANK), F32),
            jax.ShapeDtypeStruct((share, D), F32),
        ],
        compiler_params=PARAMS,
    )(grad, carried, table_new)
    return dq, new_momentum[None], weight_step[None]


def solution(mesh):
    in_specs = (
        P("ctx", "head"),
        P("ctx", "head"),
        P("ctx", "head"),
        P("ctx", "head"),
        P("ctx", "head"),
        P(),
        P(),
        P(),
        P("head", "ctx", None),
    )
    out_specs = (P("ctx", "head"), P("head", "ctx", None), P("head", "ctx", None))
    return jax.shard_map(local, mesh=mesh, in_specs=in_specs, out_specs=out_specs, check_vma=False)
```

```python
import functools
import math

import jax
import jax.numpy as jnp
from jax import lax
from jax.experimental import pallas as pl
from jax.experimental.pallas import tpu as pltpu
from jax.sharding import PartitionSpec as P

D = 4096
HEAD_SIZE = 128
GROUP = 4
BLK = 64
RAND = 3
GLOB = 2
RANK = 256
CAP = 2
ROWS = 16
PARTS = BLK // ROWS
F32 = jnp.float32
BF16 = jnp.bfloat16
VMEM = pl.BlockSpec(memory_space=pltpu.VMEM)
ANY = pl.BlockSpec(memory_space=pl.ANY)
SMEM = pl.BlockSpec(memory_space=pltpu.SMEM)
PARAMS = pltpu.CompilerParams(vmem_limit_bytes=16 * 1024 * 1024)
LARGE = pltpu.CompilerParams(vmem_limit_bytes=30 * 1024 * 1024)


def proj_table(code_value, rank_ids, feature_ids):
    row_ids = rank_ids[:, None]
    col_ids = feature_ids[None, :]
    section_one = (row_ids * 31337 + col_ids * 7919 + code_value * 10007) % 65521
    section_two = (section_one * 181 + section_one % 251 * 4093 + col_ids) % 65521
    section_three = (section_two * (section_two % 127 + 1) + row_ids * 17) % 65521
    unit_value = (section_three.astype(jnp.float32) + 0.5) / 65521.0 - 0.5
    return (unit_value * math.sqrt(12.0 / D)).astype(jnp.bfloat16)


def dot(a, b, da, db):
    return lax.dot_general(a, b, (((da,), (db,)), ((), ())), preferred_element_type=F32)


def split3(x):
    high = x.astype(BF16)
    rest = x - high.astype(F32)
    mid = rest.astype(BF16)
    return high, mid, (rest - mid.astype(F32)).astype(BF16)


def pack_kv(src_ref, k_ref, v_ref, out_ref):
    here = out_ref.shape[0]
    first = pl.program_id(0) * here
    for i in range(here):
        for c in range(CAP):
            rows = pl.ds(pl.multiple_of(src_ref[(first + i) * CAP + c] * BLK, BLK), BLK)
            out_ref[i, 2 * c * BLK : (2 * c + 1) * BLK] = k_ref[rows, :]
            out_ref[i, (2 * c + 1) * BLK : (2 * c + 2) * BLK] = v_ref[rows, :]


def add_tile(owner_ref, packed_ref, tile_ref, out_ref, wide, sem):
    tile = tile_ref[owner_ref[0], CAP + 1]
    for i in range(wide.shape[0]):
        wide[i] = tile
    copy = pltpu.make_async_copy(wide, out_ref.at[:, pl.ds(2 * CAP * BLK, ROWS), :], sem)
    copy.start()
    copy.wait()


def project(x_ref, t_ref, out_ref):
    blocks = out_ref.shape[1]
    y = dot(x_ref[...], t_ref[...], 1, 1).astype(out_ref.dtype)
    for b in range(blocks):
        for part in range(PARTS):
            row = b * BLK + part * ROWS
            for half in range(2):
                out_ref[half * PARTS + part, b] = y[row : row + ROWS, half * 128 : half * 128 + 128]


def sum_pack(src_ref, gid_ref, x_ref, k_ref, v_ref, own_ref, out_ref, acc):
    own = x_ref[0].astype(F32)
    for i in range(1, x_ref.shape[0]):
        own = own + x_ref[i].astype(F32)
    acc[...] = own.astype(BF16)
    own_ref[...] = acc[...]
    for i in range(out_ref.shape[0]):
        for c in range(CAP):
            out_ref[i, c] = acc[src_ref[i * CAP + c]]
        out_ref[i, CAP] = acc[gid_ref[i % GLOB]]
        if i < 2 * GLOB * PARTS:
            row = gid_ref[i // (2 * PARTS)] * BLK + i % PARTS * ROWS
            ref = (k_ref, v_ref)[i // PARTS % 2]
            out_ref[i, CAP + 1] = ref[pl.ds(pl.multiple_of(row, ROWS), ROWS), :]
        else:
            out_ref[i, CAP + 1] = jnp.zeros((ROWS, 128), BF16)


def collect(arrival_ref, core_ref, own_ref, before_ref, after_ref, here_ref, there_ref, recv_ref, out_ref):
    blocks = own_ref.shape[0]
    tiles = [before_ref[...]] + [own_ref[b] for b in range(blocks)] + [after_ref[...]]
    tiles += [jnp.where(core_ref[0] == g, here_ref[...], there_ref[...]) for g in range(GLOB)]
    tiles += [recv_ref[arrival_ref[n] // CAP, arrival_ref[n] % CAP] for n in range(blocks * RAND)]
    for n, tile in enumerate(tiles):
        out_ref[n] = tile


def attend(
    arrival_ref, edge_ref, from_ref, q_ref, g_ref, k_ref, v_ref, before_ref, after_ref, recv_ref, *refs
):
    dq_ref, out_ref, kwin, vwin, kglob, vglob, wacc, gacc, kg_ref, total = refs[-10:]
    tile_refs = refs[:-12]
    step, steps = pl.program_id(0), pl.num_programs(0)
    tokens = k_ref.shape[0]
    blocks = tokens // BLK
    unroll = q_ref.shape[0] // BLK
    scaling = 1.0 / math.sqrt(HEAD_SIZE)
    h = HEAD_SIZE

    @pl.when(step == 0)
    def _():
        for win, ref, low in ((kwin, k_ref, 0), (vwin, v_ref, h)):
            win[:BLK] = before_ref[:, low : low + h]
            win[BLK : BLK + tokens] = ref[...]
            win[BLK + tokens :] = after_ref[:, low : low + h]
        for kind, ref in enumerate((kglob, vglob)):
            for g in range(GLOB):
                for part in range(PARTS):
                    tile = recv_ref[(2 * g + kind) * PARTS + part, 2 * CAP * BLK :]
                    ref[g * BLK + part * ROWS : g * BLK + (part + 1) * ROWS] = tile
        wacc[...] = jnp.zeros_like(wacc)
        gacc[...] = jnp.zeros_like(gacc)

    for u in range(unroll):
        b = step * unroll + u
        rows = pl.ds(pl.multiple_of(b * BLK, BLK), 3 * BLK)
        picks = [arrival_ref[b * RAND + r] for r in range(RAND)]
        at = [(p // CAP, pl.multiple_of(p % CAP * (2 * BLK), BLK)) for p in picks]
        k_all = jnp.concatenate([kwin[rows, :]] + [recv_ref[o, pl.ds(i, BLK), :] for o, i in at] + [kglob[...]], axis=0)
        v_all = jnp.concatenate(
            [vwin[rows, :]] + [recv_ref[o, pl.ds(i + BLK, BLK), :] for o, i in at] + [vglob[...]], axis=0
        )
        here = slice(u * BLK, (u + 1) * BLK)
        q = jnp.concatenate([q_ref[here, j * h : (j + 1) * h] for j in range(GROUP)], axis=0)
        g = jnp.concatenate([g_ref[here, j * h : (j + 1) * h] for j in range(GROUP)], axis=0)
        s = dot(k_all, q, 1, 1) * (scaling * math.log2(math.e))
        left = jnp.where(b == 0, edge_ref[0], 0).astype(F32) * -1e30
        right = jnp.where(b == blocks - 1, edge_ref[1], 0).astype(F32) * -1e30
        s = jnp.concatenate(
            [s[:BLK] + left, s[BLK : 2 * BLK], s[2 * BLK : 3 * BLK] + right, s[3 * BLK :]], axis=0
        )
        e = jnp.exp2(s - jnp.max(s, axis=0, keepdims=True))
        w = e * (1.0 / jnp.sum(e, axis=0, keepdims=True))
        w_bf = w.astype(BF16)
        dw = dot(v_all, g, 1, 1)
        delta = jnp.sum(w_bf.astype(F32) * dw, axis=0, keepdims=True)
        ds = (w * (dw - delta)).astype(BF16)
        dq = jnp.transpose(dot(k_all, ds, 0, 0) * scaling).astype(BF16)
        for j in range(GROUP):
            dq_ref[here, j * h : (j + 1) * h] = dq[j * BLK : (j + 1) * BLK]
        kg = dot(ds, q, 1, 0) * scaling
        vg = dot(w_bf, g, 1, 0)
        wacc[rows, :h] += kg[: 3 * BLK]
        wacc[rows, h:] += vg[: 3 * BLK]
        gacc[:, :h] += kg[(3 + RAND) * BLK :]
        gacc[:, h:] += vg[(3 + RAND) * BLK :]
        for r in range(RAND):
            for part in range(PARTS):
                low = (3 + r) * BLK + part * ROWS
                place = blocks + 2 + GLOB + b * RAND + r
                kg_ref[part, place, :, :h] = kg[low : low + ROWS].astype(BF16)
                kg_ref[part, place, :, h:] = vg[low : low + ROWS].astype(BF16)

    @pl.when(step == steps - 1)
    def _():
        for acc, first, count in ((wacc, 0, blocks + 2), (gacc, blocks + 2, GLOB)):
            for n in range(count):
                for part in range(PARTS):
                    low = n * BLK + part * ROWS
                    kg_ref[part, first + n] = acc[low : low + ROWS, :].astype(BF16)
        total[...] = jnp.zeros_like(total)
        many = kg_ref.shape[1] * ROWS
        for i, ref in enumerate(tile_refs):
            head = from_ref[i]
            kg = kg_ref[head % PARTS].reshape(many, 2 * h)
            total[head // PARTS] += dot(kg, ref[...].reshape(many, 128), 0, 0)
        rows = total.shape[1] // out_ref.shape[0]
        for d in range(out_ref.shape[0]):
            for half in range(2):
                out_ref[d, half * rows : (half + 1) * rows] = total[half, d * rows : (d + 1) * rows]


def carry(m_ref, old_ref, new_ref, out_ref):
    rows = m_ref.shape[0]
    x = dot(jnp.concatenate(split3(m_ref[...]), axis=0), old_ref[...], 1, 0)
    x = x[:rows] + x[rows : 2 * rows] + x[2 * rows :]
    y = dot(jnp.concatenate(split3(x), axis=0), new_ref[...], 1, 1)
    out_ref[...] = 0.9 * (y[:rows] + y[rows : 2 * rows] + y[2 * rows :])


def finish(scale, recv_ref, carried_ref, new_ref, mom_ref, step_ref):
    rows = mom_ref.shape[0]
    grad = jnp.sum(recv_ref[...], axis=0) * scale
    total = carried_ref[:rows] + jnp.concatenate([grad[:rows], grad[rows:]], axis=1)
    mom_ref[...] = total
    padded = jnp.concatenate([total, jnp.zeros((8 - rows, RANK), F32)], axis=0)
    y = dot(jnp.concatenate(split3(padded), axis=0), new_ref[...], 1, 0)
    step_ref[...] = (y[:8] + y[8:16] + y[16:])[:rows]


def local(queries, keys, values, d_attn, inputs, random_ids, global_ids, step_codes, momentum):
    tokens = queries.shape[0]
    blocks = tokens // BLK
    ctx, heads = lax.axis_size("ctx"), lax.axis_size("head")
    my_ctx, my_head = lax.axis_index("ctx"), lax.axis_index("head")
    requests = blocks * RAND
    places = blocks + 2 + GLOB + requests
    h = HEAD_SIZE
    up = [(i, i + 1) for i in range(ctx - 1)]
    down = [(i + 1, i) for i in range(ctx - 1)]

    ids = random_ids.reshape(ctx, requests)
    owners, inner = ids // blocks, ids % blocks
    order = jnp.arange(requests, dtype=jnp.int32)
    tagged = order[None, :] * blocks + inner
    mine = owners == my_ctx
    first = jnp.min(jnp.where(mine, tagged, requests * blocks), axis=1) % blocks
    last = jnp.max(jnp.where(mine, tagged, 0), axis=1) % blocks
    sources = jnp.stack([first, last], axis=1).reshape(-1)
    my_owners = lax.dynamic_index_in_dim(owners, my_ctx, 0, keepdims=False)
    earlier = (my_owners[:, None] == my_owners[None, :]) & (order[None, :] < order[:, None])
    arrival = my_owners * CAP + jnp.any(earlier, axis=1).astype(jnp.int32)
    global_owner, global_inner = global_ids // blocks, global_ids % blocks

    feature_ids = my_head * inputs.shape[1] + jnp.arange(inputs.shape[1], dtype=jnp.int32)
    rank_ids = jnp.arange(RANK, dtype=jnp.int32)
    table_part = proj_table(step_codes[1], rank_ids, feature_ids)
    terms = pl.pallas_call(
        project,
        in_specs=[VMEM] * 2,
        out_specs=VMEM,
        out_shape=jax.ShapeDtypeStruct((heads, blocks, ROWS, 128), BF16),
        compiler_params=PARAMS,
    )(inputs, table_part)
    terms = lax.all_to_all(terms, "head", 0, 0, tiled=True)

    chunk = 8
    span = 2 * CAP * BLK + ROWS
    kv_out = pl.pallas_call(
        pack_kv,
        grid_spec=pltpu.PrefetchScalarGridSpec(
            num_scalar_prefetch=1,
            grid=(ctx // chunk,),
            in_specs=[VMEM] * 2,
            out_specs=pl.BlockSpec((chunk, 2 * CAP * BLK, h), lambda i, s: (i, 0, 0)),
        ),
        out_shape=pltpu.HBM((ctx, span, h), BF16),
        compiler_params=PARAMS,
    )(sources, keys, values)
    terms, kv_out = lax.optimization_barrier((terms, kv_out))
    own, p_out = pl.pallas_call(
        sum_pack,
        in_specs=[SMEM, SMEM] + [VMEM] * 3,
        out_specs=[VMEM] * 2,
        out_shape=[
            jax.ShapeDtypeStruct((blocks, ROWS, 128), BF16),
            jax.ShapeDtypeStruct((ctx, CAP + 2, ROWS, 128), BF16),
        ],
        scratch_shapes=[pltpu.VMEM((blocks, ROWS, 128), BF16)],
        compiler_params=PARAMS,
    )(sources, global_inner, terms, keys, values)

    kv_before = lax.ppermute(jnp.concatenate([keys[-BLK:], values[-BLK:]], axis=1), "ctx", up)
    kv_after = lax.ppermute(jnp.concatenate([keys[:BLK], values[:BLK]], axis=1), "ctx", down)
    p_in = lax.all_to_all(p_out, "ctx", 0, 0, tiled=True)
    p_before = lax.ppermute(own[-1], "ctx", up)
    p_after = lax.ppermute(own[0], "ctx", down)

    core = my_ctx % GLOB
    p_here = lax.dynamic_index_in_dim(p_in[:, CAP], global_owner[core], 0, keepdims=False)
    p_there = lax.ppermute(p_here, "ctx", [(i, i ^ 1) for i in range(ctx)])

    tile_owner = global_owner[jnp.minimum(my_ctx // (2 * PARTS), GLOB - 1)]
    kv_out = pl.pallas_call(
        add_tile,
        in_specs=[SMEM, ANY, VMEM],
        out_specs=ANY,
        out_shape=pltpu.HBM(kv_out.shape, BF16),
        input_output_aliases={1: 0},
        scratch_shapes=[pltpu.VMEM((ctx, ROWS, h), BF16), pltpu.SemaphoreType.DMA],
        compiler_params=PARAMS,
    )(tile_owner.reshape(1), kv_out, p_in)
    kv_out, kv_before, kv_after, p_before, p_after = lax.optimization_barrier(
        (kv_out, kv_before, kv_after, p_before, p_after)
    )
    kv_in = lax.all_to_all(kv_out, "ctx", 0, 0, tiled=True)

    tiles = pl.pallas_call(
        collect,
        in_specs=[SMEM, SMEM] + [VMEM] * 6,
        out_specs=VMEM,
        out_shape=jax.ShapeDtypeStruct((places, ROWS, 128), BF16),
        compiler_params=PARAMS,
    )(arrival, core.reshape(1), own, p_before, p_after, p_here, p_there, p_in)
    pair = [tiles, lax.ppermute(tiles, "head", [(i, i ^ 1) for i in range(heads)])]
    every = jnp.arange(D, dtype=jnp.int32)
    table_new = proj_table(step_codes[1], rank_ids, every)
    table_old = proj_table(step_codes[0], rank_ids, every)
    share = momentum.shape[1]
    carried = pl.pallas_call(
        carry,
        in_specs=[VMEM] * 3,
        out_specs=VMEM,
        out_shape=jax.ShapeDtypeStruct((8, RANK), F32),
        compiler_params=PARAMS,
    )(jnp.pad(momentum[0], ((0, 8 - share), (0, 0))), table_old, table_new)

    pair[1], carried = lax.optimization_barrier((pair[1], carried))
    all_tiles, all_heads = list(pair), [my_head, my_head ^ 1]
    for far in range(2, heads, 2):
        there = [(i, (i + far) % heads) for i in range(heads)]
        all_tiles += [lax.ppermute(t, "head", there) for t in pair]
        source = (my_head - far) % heads
        all_heads += [source, source ^ 1]

    edges = jnp.stack([my_ctx == 0, my_ctx == ctx - 1]).astype(jnp.int32)
    unroll = 8
    wide = pl.BlockSpec((unroll * BLK, GROUP * h), lambda i: (i, 0))
    queries, d_attn = (pltpu.with_memory_space_constraint(x, pltpu.HBM) for x in (queries, d_attn))
    dq, grad = pl.pallas_call(
        attend,
        grid=(blocks // unroll,),
        in_specs=[SMEM] * 3 + [wide] * 2 + [VMEM] * (5 + heads) + [ANY] * 2,
        out_specs=[wide, VMEM],
        out_shape=[
            jax.ShapeDtypeStruct((tokens, GROUP * h), BF16),
            pltpu.HBM((ctx, 2 * share, 128), F32),
        ],
        scratch_shapes=[
            pltpu.VMEM((tokens + 2 * BLK, h), BF16),
            pltpu.VMEM((tokens + 2 * BLK, h), BF16),
            pltpu.VMEM((GLOB * BLK, h), BF16),
            pltpu.VMEM((GLOB * BLK, h), BF16),
            pltpu.VMEM((tokens + 2 * BLK, 2 * h), F32),
            pltpu.VMEM((GLOB * BLK, 2 * h), F32),
            pltpu.VMEM((PARTS, places, ROWS, 2 * h), BF16),
            pltpu.VMEM((2, 2 * h, 128), F32),
        ],
        compiler_params=LARGE,
    )(
        arrival, edges, jnp.stack(all_heads), queries, d_attn, keys, values, kv_before, kv_after, kv_in,
        *all_tiles, table_new, carried,
    )
    grad = lax.all_to_all(grad, "ctx", 0, 0, tiled=True)
    new_momentum, weight_step = pl.pallas_call(
        functools.partial(finish, 1.0 / math.sqrt(tokens * ctx)),
        in_specs=[VMEM] * 3,
        out_specs=[VMEM] * 2,
        out_shape=[
            jax.ShapeDtypeStruct((share, RANK), F32),
            jax.ShapeDtypeStruct((share, D), F32),
        ],
        compiler_params=PARAMS,
    )(grad, carried, table_new)
    return dq, new_momentum[None], weight_step[None]


def solution(mesh):
    in_specs = (
        P("ctx", "head"),
        P("ctx", "head"),
        P("ctx", "head"),
        P("ctx", "head"),
        P("ctx", "head"),
        P(),
        P(),
        P(),
        P("head", "ctx", None),
    )
    out_specs = (P("ctx", "head"), P("head", "ctx", None), P("head", "ctx", None))
    return jax.shard_map(local, mesh=mesh, in_specs=in_specs, out_specs=out_specs, check_vma=False)
```

```python
import functools
import math

import jax
import jax.numpy as jnp
from jax import lax
from jax.experimental import pallas as pl
from jax.experimental.pallas import tpu as pltpu
from jax.sharding import PartitionSpec as P

D = 4096
HEAD_SIZE = 128
GROUP = 4
BLK = 64
RAND = 3
GLOB = 2
RANK = 256
CAP = 2
ROWS = 16
PARTS = BLK // ROWS
F32 = jnp.float32
BF16 = jnp.bfloat16
VMEM = pl.BlockSpec(memory_space=pltpu.VMEM)
ANY = pl.BlockSpec(memory_space=pl.ANY)
SMEM = pl.BlockSpec(memory_space=pltpu.SMEM)
PARAMS = pltpu.CompilerParams(vmem_limit_bytes=16 * 1024 * 1024)
LARGE = pltpu.CompilerParams(vmem_limit_bytes=30 * 1024 * 1024)


def proj_table(code_value, rank_ids, feature_ids):
    row_ids = rank_ids[:, None]
    col_ids = feature_ids[None, :]
    section_one = (row_ids * 31337 + col_ids * 7919 + code_value * 10007) % 65521
    section_two = (section_one * 181 + section_one % 251 * 4093 + col_ids) % 65521
    section_three = (section_two * (section_two % 127 + 1) + row_ids * 17) % 65521
    unit_value = (section_three.astype(jnp.float32) + 0.5) / 65521.0 - 0.5
    return (unit_value * math.sqrt(12.0 / D)).astype(jnp.bfloat16)


def dot(a, b, da, db):
    return lax.dot_general(a, b, (((da,), (db,)), ((), ())), preferred_element_type=F32)


def split3(x):
    high = x.astype(BF16)
    rest = x - high.astype(F32)
    mid = rest.astype(BF16)
    return high, mid, (rest - mid.astype(F32)).astype(BF16)


def pack_kv(src_ref, k_ref, v_ref, out_ref):
    here = out_ref.shape[0]
    first = pl.program_id(0) * here
    for i in range(here):
        for c in range(CAP):
            rows = pl.ds(pl.multiple_of(src_ref[(first + i) * CAP + c] * BLK, BLK), BLK)
            out_ref[i, 2 * c * BLK : (2 * c + 1) * BLK] = k_ref[rows, :]
            out_ref[i, (2 * c + 1) * BLK : (2 * c + 2) * BLK] = v_ref[rows, :]


def add_tile(owner_ref, packed_ref, tile_ref, out_ref, wide, sem):
    tile = tile_ref[owner_ref[0], CAP + 1]
    for i in range(wide.shape[0]):
        wide[i] = tile
    copy = pltpu.make_async_copy(wide, out_ref.at[:, pl.ds(2 * CAP * BLK, ROWS), :], sem)
    copy.start()
    copy.wait()


def project(x_ref, t_ref, out_ref):
    blocks = out_ref.shape[1]
    y = dot(x_ref[...], t_ref[...], 1, 1).astype(out_ref.dtype)
    for b in range(blocks):
        for part in range(PARTS):
            row = b * BLK + part * ROWS
            for half in range(2):
                out_ref[half * PARTS + part, b] = y[row : row + ROWS, half * 128 : half * 128 + 128]


def sum_pack(src_ref, gid_ref, x_ref, k_ref, v_ref, own_ref, out_ref, acc):
    own = x_ref[0].astype(F32)
    for i in range(1, x_ref.shape[0]):
        own = own + x_ref[i].astype(F32)
    acc[...] = own.astype(BF16)
    own_ref[...] = acc[...]
    for i in range(out_ref.shape[0]):
        for c in range(CAP):
            out_ref[i, c] = acc[src_ref[i * CAP + c]]
        out_ref[i, CAP] = acc[gid_ref[i % GLOB]]
        if i < 2 * GLOB * PARTS:
            row = gid_ref[i // (2 * PARTS)] * BLK + i % PARTS * ROWS
            ref = (k_ref, v_ref)[i // PARTS % 2]
            out_ref[i, CAP + 1] = ref[pl.ds(pl.multiple_of(row, ROWS), ROWS), :]
        else:
            out_ref[i, CAP + 1] = jnp.zeros((ROWS, 128), BF16)


def collect(arrival_ref, core_ref, before_ref, after_ref, here_ref, there_ref, recv_ref, out_ref):
    tiles = [before_ref[...], after_ref[...]]
    tiles += [jnp.where(core_ref[0] == g, here_ref[...], there_ref[...]) for g in range(GLOB)]
    tiles += [recv_ref[arrival_ref[n] // CAP, arrival_ref[n] % CAP] for n in range(arrival_ref.shape[0])]
    for n, tile in enumerate(tiles):
        out_ref[n] = tile


def attend(
    arrival_ref, edge_ref, from_ref, q_ref, g_ref, k_ref, v_ref, before_ref, after_ref, recv_ref, *refs
):
    dq_ref, out_ref, kwin, vwin, kglob, vglob, wacc, gacc, kg_ref, total = refs[-10:]
    tile_refs = refs[:-12]
    step, steps = pl.program_id(0), pl.num_programs(0)
    tokens = k_ref.shape[0]
    blocks = tokens // BLK
    unroll = q_ref.shape[0] // BLK
    scaling = 1.0 / math.sqrt(HEAD_SIZE)
    h = HEAD_SIZE

    @pl.when(step == 0)
    def _():
        for win, ref, low in ((kwin, k_ref, 0), (vwin, v_ref, h)):
            win[:BLK] = before_ref[:, low : low + h]
            win[BLK : BLK + tokens] = ref[...]
            win[BLK + tokens :] = after_ref[:, low : low + h]
        for kind, ref in enumerate((kglob, vglob)):
            for g in range(GLOB):
                for part in range(PARTS):
                    tile = recv_ref[(2 * g + kind) * PARTS + part, 2 * CAP * BLK :]
                    ref[g * BLK + part * ROWS : g * BLK + (part + 1) * ROWS] = tile
        wacc[...] = jnp.zeros_like(wacc)
        gacc[...] = jnp.zeros_like(gacc)

    for u in range(unroll):
        b = step * unroll + u
        rows = pl.ds(pl.multiple_of(b * BLK, BLK), 3 * BLK)
        picks = [arrival_ref[b * RAND + r] for r in range(RAND)]
        at = [(p // CAP, pl.multiple_of(p % CAP * (2 * BLK), BLK)) for p in picks]
        k_all = jnp.concatenate([kwin[rows, :]] + [recv_ref[o, pl.ds(i, BLK), :] for o, i in at] + [kglob[...]], axis=0)
        v_all = jnp.concatenate(
            [vwin[rows, :]] + [recv_ref[o, pl.ds(i + BLK, BLK), :] for o, i in at] + [vglob[...]], axis=0
        )
        here = slice(u * BLK, (u + 1) * BLK)
        q = jnp.concatenate([q_ref[here, j * h : (j + 1) * h] for j in range(GROUP)], axis=0)
        g = jnp.concatenate([g_ref[here, j * h : (j + 1) * h] for j in range(GROUP)], axis=0)
        s = dot(k_all, q, 1, 1) * (scaling * math.log2(math.e))
        left = jnp.where(b == 0, edge_ref[0], 0).astype(F32) * -1e30
        right = jnp.where(b == blocks - 1, edge_ref[1], 0).astype(F32) * -1e30
        s = jnp.concatenate(
            [s[:BLK] + left, s[BLK : 2 * BLK], s[2 * BLK : 3 * BLK] + right, s[3 * BLK :]], axis=0
        )
        e = jnp.exp2(s - jnp.max(s, axis=0, keepdims=True))
        w = e * (1.0 / jnp.sum(e, axis=0, keepdims=True))
        w_bf = w.astype(BF16)
        dw = dot(v_all, g, 1, 1)
        delta = jnp.sum(w_bf.astype(F32) * dw, axis=0, keepdims=True)
        ds = (w * (dw - delta)).astype(BF16)
        dq = jnp.transpose(dot(k_all, ds, 0, 0) * scaling).astype(BF16)
        for j in range(GROUP):
            dq_ref[here, j * h : (j + 1) * h] = dq[j * BLK : (j + 1) * BLK]
        kg = dot(ds, q, 1, 0) * scaling
        vg = dot(w_bf, g, 1, 0)
        wacc[rows, :h] += kg[: 3 * BLK]
        wacc[rows, h:] += vg[: 3 * BLK]
        gacc[:, :h] += kg[(3 + RAND) * BLK :]
        gacc[:, h:] += vg[(3 + RAND) * BLK :]
        for r in range(RAND):
            for part in range(PARTS):
                low = (3 + r) * BLK + part * ROWS
                place = blocks + 2 + GLOB + b * RAND + r
                kg_ref[part, place, :, :h] = kg[low : low + ROWS].astype(BF16)
                kg_ref[part, place, :, h:] = vg[low : low + ROWS].astype(BF16)

    @pl.when(step == steps - 1)
    def _():
        window = [(wacc, n + 1, n) for n in range(blocks)] + [(wacc, 0, blocks), (wacc, blocks + 1, blocks + 1)]
        for acc, n, place in window + [(gacc, n, blocks + 2 + n) for n in range(GLOB)]:
            for part in range(PARTS):
                low = n * BLK + part * ROWS
                kg_ref[part, place] = acc[low : low + ROWS, :].astype(BF16)
        total[...] = jnp.zeros_like(total)
        many = kg_ref.shape[1] * ROWS
        for i in range(from_ref.shape[0]):
            head = from_ref[i]
            own, other = tile_refs[i // 2], tile_refs[from_ref.shape[0] // 2 + i]
            kg = kg_ref[head % PARTS].reshape(many, 2 * h)
            tile = jnp.concatenate([own[i % 2].reshape(blocks * ROWS, 128), other[...].reshape(-1, 128)], axis=0)
            total[head // PARTS] += dot(kg, tile, 0, 0)
        rows = total.shape[1] // out_ref.shape[0]
        for d in range(out_ref.shape[0]):
            for half in range(2):
                out_ref[d, half * rows : (half + 1) * rows] = total[half, d * rows : (d + 1) * rows]


def carry(m_ref, old_ref, new_ref, out_ref):
    rows = m_ref.shape[0]
    x = dot(jnp.concatenate(split3(m_ref[...]), axis=0), old_ref[...], 1, 0)
    x = x[:rows] + x[rows : 2 * rows] + x[2 * rows :]
    y = dot(jnp.concatenate(split3(x), axis=0), new_ref[...], 1, 1)
    out_ref[...] = 0.9 * (y[:rows] + y[rows : 2 * rows] + y[2 * rows :])


def finish(scale, recv_ref, carried_ref, new_ref, mom_ref, step_ref):
    rows = mom_ref.shape[0]
    grad = jnp.sum(recv_ref[...], axis=0) * scale
    total = carried_ref[:rows] + jnp.concatenate([grad[:rows], grad[rows:]], axis=1)
    mom_ref[...] = total
    padded = jnp.concatenate([total, jnp.zeros((8 - rows, RANK), F32)], axis=0)
    y = dot(jnp.concatenate(split3(padded), axis=0), new_ref[...], 1, 0)
    step_ref[...] = (y[:8] + y[8:16] + y[16:])[:rows]


def local(queries, keys, values, d_attn, inputs, random_ids, global_ids, step_codes, momentum):
    tokens = queries.shape[0]
    blocks = tokens // BLK
    ctx, heads = lax.axis_size("ctx"), lax.axis_size("head")
    my_ctx, my_head = lax.axis_index("ctx"), lax.axis_index("head")
    requests = blocks * RAND
    places = blocks + 2 + GLOB + requests
    h = HEAD_SIZE
    up = [(i, i + 1) for i in range(ctx - 1)]
    down = [(i + 1, i) for i in range(ctx - 1)]

    ids = random_ids.reshape(ctx, requests)
    owners, inner = ids // blocks, ids % blocks
    order = jnp.arange(requests, dtype=jnp.int32)
    tagged = order[None, :] * blocks + inner
    mine = owners == my_ctx
    first = jnp.min(jnp.where(mine, tagged, requests * blocks), axis=1) % blocks
    last = jnp.max(jnp.where(mine, tagged, 0), axis=1) % blocks
    sources = jnp.stack([first, last], axis=1).reshape(-1)
    my_owners = lax.dynamic_index_in_dim(owners, my_ctx, 0, keepdims=False)
    earlier = (my_owners[:, None] == my_owners[None, :]) & (order[None, :] < order[:, None])
    arrival = my_owners * CAP + jnp.any(earlier, axis=1).astype(jnp.int32)
    global_owner, global_inner = global_ids // blocks, global_ids % blocks

    feature_ids = my_head * inputs.shape[1] + jnp.arange(inputs.shape[1], dtype=jnp.int32)
    rank_ids = jnp.arange(RANK, dtype=jnp.int32)
    table_part = proj_table(step_codes[1], rank_ids, feature_ids)
    terms = pl.pallas_call(
        project,
        in_specs=[VMEM] * 2,
        out_specs=VMEM,
        out_shape=jax.ShapeDtypeStruct((heads, blocks, ROWS, 128), BF16),
        compiler_params=PARAMS,
    )(inputs, table_part)
    terms = lax.all_to_all(terms, "head", 0, 0, tiled=True)

    chunk = 8
    span = 2 * CAP * BLK + ROWS
    kv_out = pl.pallas_call(
        pack_kv,
        grid_spec=pltpu.PrefetchScalarGridSpec(
            num_scalar_prefetch=1,
            grid=(ctx // chunk,),
            in_specs=[VMEM] * 2,
            out_specs=pl.BlockSpec((chunk, 2 * CAP * BLK, h), lambda i, s: (i, 0, 0)),
        ),
        out_shape=pltpu.HBM((ctx, span, h), BF16),
        compiler_params=PARAMS,
    )(sources, keys, values)
    terms, kv_out = lax.optimization_barrier((terms, kv_out))
    own, p_out = pl.pallas_call(
        sum_pack,
        in_specs=[SMEM, SMEM] + [VMEM] * 3,
        out_specs=[VMEM] * 2,
        out_shape=[
            jax.ShapeDtypeStruct((blocks, ROWS, 128), BF16),
            jax.ShapeDtypeStruct((ctx, CAP + 2, ROWS, 128), BF16),
        ],
        scratch_shapes=[pltpu.VMEM((blocks, ROWS, 128), BF16)],
        compiler_params=PARAMS,
    )(sources, global_inner, terms, keys, values)

    kv_before = lax.ppermute(jnp.concatenate([keys[-BLK:], values[-BLK:]], axis=1), "ctx", up)
    kv_after = lax.ppermute(jnp.concatenate([keys[:BLK], values[:BLK]], axis=1), "ctx", down)
    across = [(i, i ^ 1) for i in range(heads)]
    own_pair = jnp.stack([own, lax.ppermute(own, "head", across)])
    p_in = lax.all_to_all(p_out, "ctx", 0, 0, tiled=True)
    p_before = lax.ppermute(own[-1], "ctx", up)
    p_after = lax.ppermute(own[0], "ctx", down)

    core = my_ctx % GLOB
    p_here = lax.dynamic_index_in_dim(p_in[:, CAP], global_owner[core], 0, keepdims=False)
    p_there = lax.ppermute(p_here, "ctx", [(i, i ^ 1) for i in range(ctx)])

    tile_owner = global_owner[jnp.minimum(my_ctx // (2 * PARTS), GLOB - 1)]
    kv_out = pl.pallas_call(
        add_tile,
        in_specs=[SMEM, ANY, VMEM],
        out_specs=ANY,
        out_shape=pltpu.HBM(kv_out.shape, BF16),
        input_output_aliases={1: 0},
        scratch_shapes=[pltpu.VMEM((ctx, ROWS, h), BF16), pltpu.SemaphoreType.DMA],
        compiler_params=PARAMS,
    )(tile_owner.reshape(1), kv_out, p_in)
    kv_out, kv_before, kv_after, p_before, p_after, own_pair = lax.optimization_barrier(
        (kv_out, kv_before, kv_after, p_before, p_after, own_pair)
    )
    kv_in = lax.all_to_all(kv_out, "ctx", 0, 0, tiled=True)

    tiles = pl.pallas_call(
        collect,
        in_specs=[SMEM, SMEM] + [VMEM] * 5,
        out_specs=VMEM,
        out_shape=jax.ShapeDtypeStruct((places - blocks, ROWS, 128), BF16),
        compiler_params=PARAMS,
    )(arrival, core.reshape(1), p_before, p_after, p_here, p_there, p_in)
    pair = [tiles, lax.ppermute(tiles, "head", across)]
    every = jnp.arange(D, dtype=jnp.int32)
    table_new = proj_table(step_codes[1], rank_ids, every)
    table_old = proj_table(step_codes[0], rank_ids, every)
    own_pair, table_new = lax.optimization_barrier((own_pair, table_new))
    share = momentum.shape[1]
    carried = pl.pallas_call(
        carry,
        in_specs=[VMEM] * 3,
        out_specs=VMEM,
        out_shape=jax.ShapeDtypeStruct((8, RANK), F32),
        compiler_params=PARAMS,
    )(jnp.pad(momentum[0], ((0, 8 - share), (0, 0))), table_old, table_new)

    pair[1], carried = lax.optimization_barrier((pair[1], carried))
    own_tiles, all_tiles, all_heads = [own_pair], list(pair), [my_head, my_head ^ 1]
    for far in range(2, heads, 2):
        there = [(i, (i + far) % heads) for i in range(heads)]
        own_tiles.append(lax.ppermute(own_pair, "head", there))
        all_tiles += [lax.ppermute(t, "head", there) for t in pair]
        source = (my_head - far) % heads
        all_heads += [source, source ^ 1]

    edges = jnp.stack([my_ctx == 0, my_ctx == ctx - 1]).astype(jnp.int32)
    unroll = 8
    wide = pl.BlockSpec((unroll * BLK, GROUP * h), lambda i: (i, 0))
    queries, d_attn = (pltpu.with_memory_space_constraint(x, pltpu.HBM) for x in (queries, d_attn))
    dq, grad = pl.pallas_call(
        attend,
        grid=(blocks // unroll,),
        in_specs=[SMEM] * 3 + [wide] * 2 + [VMEM] * (5 + heads // 2 + heads) + [ANY] * 2,
        out_specs=[wide, VMEM],
        out_shape=[
            jax.ShapeDtypeStruct((tokens, GROUP * h), BF16),
            pltpu.HBM((ctx, 2 * share, 128), F32),
        ],
        scratch_shapes=[
            pltpu.VMEM((tokens + 2 * BLK, h), BF16),
            pltpu.VMEM((tokens + 2 * BLK, h), BF16),
            pltpu.VMEM((GLOB * BLK, h), BF16),
            pltpu.VMEM((GLOB * BLK, h), BF16),
            pltpu.VMEM((tokens + 2 * BLK, 2 * h), F32),
            pltpu.VMEM((GLOB * BLK, 2 * h), F32),
            pltpu.VMEM((PARTS, places, ROWS, 2 * h), BF16),
            pltpu.VMEM((2, 2 * h, 128), F32),
        ],
        compiler_params=LARGE,
    )(
        arrival, edges, jnp.stack(all_heads), queries, d_attn, keys, values, kv_before, kv_after, kv_in,
        *own_tiles, *all_tiles, table_new, carried,
    )
    grad = lax.all_to_all(grad, "ctx", 0, 0, tiled=True)
    new_momentum, weight_step = pl.pallas_call(
        functools.partial(finish, 1.0 / math.sqrt(tokens * ctx)),
        in_specs=[VMEM] * 3,
        out_specs=[VMEM] * 2,
        out_shape=[
            jax.ShapeDtypeStruct((share, RANK), F32),
            jax.ShapeDtypeStruct((share, D), F32),
        ],
        compiler_params=PARAMS,
    )(grad, carried, table_new)
    return dq, new_momentum[None], weight_step[None]


def solution(mesh):
    in_specs = (
        P("ctx", "head"),
        P("ctx", "head"),
        P("ctx", "head"),
        P("ctx", "head"),
        P("ctx", "head"),
        P(),
        P(),
        P(),
        P("head", "ctx", None),
    )
    out_specs = (P("ctx", "head"), P("head", "ctx", None), P("head", "ctx", None))
    return jax.shard_map(local, mesh=mesh, in_specs=in_specs, out_specs=out_specs, check_vma=False)
```

```python
import functools
import math

import jax
import jax.numpy as jnp
from jax import lax
from jax.experimental import pallas as pl
from jax.experimental.pallas import tpu as pltpu
from jax.sharding import PartitionSpec as P

D = 4096
HEAD_SIZE = 128
GROUP = 4
BLK = 64
RAND = 3
GLOB = 2
RANK = 256
CAP = 2
ROWS = 16
PARTS = BLK // ROWS
F32 = jnp.float32
BF16 = jnp.bfloat16
VMEM = pl.BlockSpec(memory_space=pltpu.VMEM)
ANY = pl.BlockSpec(memory_space=pl.ANY)
SMEM = pl.BlockSpec(memory_space=pltpu.SMEM)
PARAMS = pltpu.CompilerParams(vmem_limit_bytes=16 * 1024 * 1024)
LARGE = pltpu.CompilerParams(vmem_limit_bytes=30 * 1024 * 1024)


def proj_table(code_value, rank_ids, feature_ids):
    row_ids = rank_ids[:, None]
    col_ids = feature_ids[None, :]
    section_one = (row_ids * 31337 + col_ids * 7919 + code_value * 10007) % 65521
    section_two = (section_one * 181 + section_one % 251 * 4093 + col_ids) % 65521
    section_three = (section_two * (section_two % 127 + 1) + row_ids * 17) % 65521
    unit_value = (section_three.astype(jnp.float32) + 0.5) / 65521.0 - 0.5
    return (unit_value * math.sqrt(12.0 / D)).astype(jnp.bfloat16)


def dot(a, b, da, db):
    return lax.dot_general(a, b, (((da,), (db,)), ((), ())), preferred_element_type=F32)


def split3(x):
    high = x.astype(BF16)
    rest = x - high.astype(F32)
    mid = rest.astype(BF16)
    return high, mid, (rest - mid.astype(F32)).astype(BF16)


def pack_kv(src_ref, k_ref, v_ref, out_ref):
    here = out_ref.shape[0]
    first = pl.program_id(0) * here
    for i in range(here):
        for c in range(CAP):
            rows = pl.ds(pl.multiple_of(src_ref[(first + i) * CAP + c] * BLK, BLK), BLK)
            out_ref[i, 2 * c * BLK : (2 * c + 1) * BLK] = k_ref[rows, :]
            out_ref[i, (2 * c + 1) * BLK : (2 * c + 2) * BLK] = v_ref[rows, :]


def add_tile(owner_ref, packed_ref, tile_ref, out_ref, wide, sem):
    tile = tile_ref[owner_ref[0], CAP + 1]
    for i in range(wide.shape[0]):
        wide[i] = tile
    copy = pltpu.make_async_copy(wide, out_ref.at[:, pl.ds(2 * CAP * BLK, ROWS), :], sem)
    copy.start()
    copy.wait()


def project(x_ref, t_ref, out_ref):
    blocks = out_ref.shape[1]
    y = dot(x_ref[...], t_ref[...], 1, 1).astype(out_ref.dtype)
    for b in range(blocks):
        for part in range(PARTS):
            row = b * BLK + part * ROWS
            for half in range(2):
                out_ref[half * PARTS + part, b] = y[row : row + ROWS, half * 128 : half * 128 + 128]


def sum_pack(src_ref, gid_ref, x_ref, k_ref, v_ref, own_ref, out_ref, acc):
    own = x_ref[0].astype(F32)
    for i in range(1, x_ref.shape[0]):
        own = own + x_ref[i].astype(F32)
    acc[...] = own.astype(BF16)
    own_ref[...] = acc[...]
    for i in range(out_ref.shape[0]):
        for c in range(CAP):
            out_ref[i, c] = acc[src_ref[i * CAP + c]]
        out_ref[i, CAP] = acc[gid_ref[i % GLOB]]
        if i < 2 * GLOB * PARTS:
            row = gid_ref[i // (2 * PARTS)] * BLK + i % PARTS * ROWS
            ref = (k_ref, v_ref)[i // PARTS % 2]
            out_ref[i, CAP + 1] = ref[pl.ds(pl.multiple_of(row, ROWS), ROWS), :]
        else:
            out_ref[i, CAP + 1] = jnp.zeros((ROWS, 128), BF16)


def collect(arrival_ref, core_ref, own_ref, before_ref, after_ref, here_ref, there_ref, recv_ref, out_ref):
    blocks = own_ref.shape[0]
    tiles = [before_ref[...]] + [own_ref[b] for b in range(blocks)] + [after_ref[...]]
    tiles += [jnp.where(core_ref[0] == g, here_ref[...], there_ref[...]) for g in range(GLOB)]
    tiles += [recv_ref[arrival_ref[n] // CAP, arrival_ref[n] % CAP] for n in range(blocks * RAND)]
    for n, tile in enumerate(tiles):
        out_ref[n] = tile


def attend(
    arrival_ref, edge_ref, from_ref, q_ref, g_ref, k_ref, v_ref, before_ref, after_ref, recv_ref, *refs
):
    dq_ref, out_ref, kwin, vwin, kglob, vglob, wacc, gacc, kg_ref, total = refs[-10:]
    tile_refs = refs[:-12]
    step, steps = pl.program_id(0), pl.num_programs(0)
    tokens = k_ref.shape[0]
    blocks = tokens // BLK
    unroll = q_ref.shape[0] // BLK
    scaling = 1.0 / math.sqrt(HEAD_SIZE)
    h = HEAD_SIZE

    @pl.when(step == 0)
    def _():
        for win, ref, low in ((kwin, k_ref, 0), (vwin, v_ref, h)):
            win[:BLK] = before_ref[:, low : low + h]
            win[BLK : BLK + tokens] = ref[...]
            win[BLK + tokens :] = after_ref[:, low : low + h]
        for kind, ref in enumerate((kglob, vglob)):
            for g in range(GLOB):
                for part in range(PARTS):
                    tile = recv_ref[(2 * g + kind) * PARTS + part, 2 * CAP * BLK :]
                    ref[g * BLK + part * ROWS : g * BLK + (part + 1) * ROWS] = tile
        wacc[...] = jnp.zeros_like(wacc)
        gacc[...] = jnp.zeros_like(gacc)

    for u in range(unroll):
        b = step * unroll + u
        rows = pl.ds(pl.multiple_of(b * BLK, BLK), 3 * BLK)
        picks = [arrival_ref[b * RAND + r] for r in range(RAND)]
        at = [(p // CAP, pl.multiple_of(p % CAP * (2 * BLK), BLK)) for p in picks]
        k_all = jnp.concatenate([kwin[rows, :]] + [recv_ref[o, pl.ds(i, BLK), :] for o, i in at] + [kglob[...]], axis=0)
        v_all = jnp.concatenate(
            [vwin[rows, :]] + [recv_ref[o, pl.ds(i + BLK, BLK), :] for o, i in at] + [vglob[...]], axis=0
        )
        here = slice(u * BLK, (u + 1) * BLK)
        q = jnp.concatenate([q_ref[here, j * h : (j + 1) * h] for j in range(GROUP)], axis=0)
        g = jnp.concatenate([g_ref[here, j * h : (j + 1) * h] for j in range(GROUP)], axis=0)
        s = dot(k_all, q, 1, 1) * (scaling * math.log2(math.e))
        left = jnp.where(b == 0, edge_ref[0], 0).astype(F32) * -1e30
        right = jnp.where(b == blocks - 1, edge_ref[1], 0).astype(F32) * -1e30
        s = jnp.concatenate(
            [s[:BLK] + left, s[BLK : 2 * BLK], s[2 * BLK : 3 * BLK] + right, s[3 * BLK :]], axis=0
        )
        e = jnp.exp2(s - jnp.max(s, axis=0, keepdims=True))
        w = e * (1.0 / jnp.sum(e, axis=0, keepdims=True))
        w_bf = w.astype(BF16)
        dw = dot(v_all, g, 1, 1)
        delta = jnp.sum(w_bf.astype(F32) * dw, axis=0, keepdims=True)
        ds = (w * (dw - delta)).astype(BF16)
        dq = jnp.transpose(dot(k_all, ds, 0, 0) * scaling).astype(BF16)
        for j in range(GROUP):
            dq_ref[here, j * h : (j + 1) * h] = dq[j * BLK : (j + 1) * BLK]
        kg = dot(ds, q, 1, 0) * scaling
        vg = dot(w_bf, g, 1, 0)
        wacc[rows, :h] += kg[: 3 * BLK]
        wacc[rows, h:] += vg[: 3 * BLK]
        gacc[:, :h] += kg[(3 + RAND) * BLK :]
        gacc[:, h:] += vg[(3 + RAND) * BLK :]
        for r in range(RAND):
            for part in range(PARTS):
                low = (3 + r) * BLK + part * ROWS
                place = blocks + 2 + GLOB + b * RAND + r
                kg_ref[part, place, :, :h] = kg[low : low + ROWS].astype(BF16)
                kg_ref[part, place, :, h:] = vg[low : low + ROWS].astype(BF16)

    @pl.when(step == steps - 1)
    def _():
        for acc, first, count in ((wacc, 0, blocks + 2), (gacc, blocks + 2, GLOB)):
            for n in range(count):
                for part in range(PARTS):
                    low = n * BLK + part * ROWS
                    kg_ref[part, first + n] = acc[low : low + ROWS, :].astype(BF16)
        total[...] = jnp.zeros_like(total)
        many = kg_ref.shape[1] * ROWS
        for i, ref in enumerate(tile_refs):
            head = from_ref[i]
            kg = kg_ref[head % PARTS].reshape(many, 2 * h)
            total[head // PARTS] += dot(kg, ref[...].reshape(many, 128), 0, 0)
        rows = total.shape[1] // out_ref.shape[0]
        for d in range(out_ref.shape[0]):
            for half in range(2):
                out_ref[d, half * rows : (half + 1) * rows] = total[half, d * rows : (d + 1) * rows]


def carry(m_ref, old_ref, new_ref, out_ref):
    rows = m_ref.shape[0]
    x = dot(jnp.concatenate(split3(m_ref[...]), axis=0), old_ref[...], 1, 0)
    x = x[:rows] + x[rows : 2 * rows] + x[2 * rows :]
    y = dot(jnp.concatenate(split3(x), axis=0), new_ref[...], 1, 1)
    out_ref[...] = 0.9 * (y[:rows] + y[rows : 2 * rows] + y[2 * rows :])


def finish(scale, recv_ref, carried_ref, new_ref, mom_ref, step_ref):
    rows = mom_ref.shape[0]
    grad = jnp.sum(recv_ref[...], axis=0) * scale
    total = carried_ref[:rows] + jnp.concatenate([grad[:rows], grad[rows:]], axis=1)
    mom_ref[...] = total
    padded = jnp.concatenate([total, jnp.zeros((8 - rows, RANK), F32)], axis=0)
    y = dot(jnp.concatenate(split3(padded), axis=0), new_ref[...], 1, 0)
    step_ref[...] = (y[:8] + y[8:16] + y[16:])[:rows]


def local(queries, keys, values, d_attn, inputs, random_ids, global_ids, step_codes, momentum):
    tokens = queries.shape[0]
    blocks = tokens // BLK
    ctx, heads = lax.axis_size("ctx"), lax.axis_size("head")
    my_ctx, my_head = lax.axis_index("ctx"), lax.axis_index("head")
    requests = blocks * RAND
    places = blocks + 2 + GLOB + requests
    h = HEAD_SIZE
    up = [(i, i + 1) for i in range(ctx - 1)]
    down = [(i + 1, i) for i in range(ctx - 1)]

    ids = random_ids.reshape(ctx, requests)
    owners, inner = ids // blocks, ids % blocks
    order = jnp.arange(requests, dtype=jnp.int32)
    tagged = order[None, :] * blocks + inner
    mine = owners == my_ctx
    first = jnp.min(jnp.where(mine, tagged, requests * blocks), axis=1) % blocks
    last = jnp.max(jnp.where(mine, tagged, 0), axis=1) % blocks
    sources = jnp.stack([first, last], axis=1).reshape(-1)
    my_owners = lax.dynamic_index_in_dim(owners, my_ctx, 0, keepdims=False)
    earlier = (my_owners[:, None] == my_owners[None, :]) & (order[None, :] < order[:, None])
    arrival = my_owners * CAP + jnp.any(earlier, axis=1).astype(jnp.int32)
    global_owner, global_inner = global_ids // blocks, global_ids % blocks

    feature_ids = my_head * inputs.shape[1] + jnp.arange(inputs.shape[1], dtype=jnp.int32)
    rank_ids = jnp.arange(RANK, dtype=jnp.int32)
    table_part = proj_table(step_codes[1], rank_ids, feature_ids)
    terms = pl.pallas_call(
        project,
        in_specs=[VMEM] * 2,
        out_specs=VMEM,
        out_shape=jax.ShapeDtypeStruct((heads, blocks, ROWS, 128), BF16),
        compiler_params=PARAMS,
    )(inputs, table_part)
    terms = lax.all_to_all(terms, "head", 0, 0, tiled=True)

    chunk = 8
    span = 2 * CAP * BLK + ROWS
    kv_out = pl.pallas_call(
        pack_kv,
        grid_spec=pltpu.PrefetchScalarGridSpec(
            num_scalar_prefetch=1,
            grid=(ctx // chunk,),
            in_specs=[VMEM] * 2,
            out_specs=pl.BlockSpec((chunk, 2 * CAP * BLK, h), lambda i, s: (i, 0, 0)),
        ),
        out_shape=pltpu.HBM((ctx, span, h), BF16),
        compiler_params=PARAMS,
    )(sources, keys, values)
    kv_before = lax.ppermute(jnp.concatenate([keys[-BLK:], values[-BLK:]], axis=1), "ctx", up)
    kv_after = lax.ppermute(jnp.concatenate([keys[:BLK], values[:BLK]], axis=1), "ctx", down)
    terms, kv_out, kv_before, kv_after = lax.optimization_barrier((terms, kv_out, kv_before, kv_after))
    own, p_out = pl.pallas_call(
        sum_pack,
        in_specs=[SMEM, SMEM] + [VMEM] * 3,
        out_specs=[VMEM] * 2,
        out_shape=[
            jax.ShapeDtypeStruct((blocks, ROWS, 128), BF16),
            jax.ShapeDtypeStruct((ctx, CAP + 2, ROWS, 128), BF16),
        ],
        scratch_shapes=[pltpu.VMEM((blocks, ROWS, 128), BF16)],
        compiler_params=PARAMS,
    )(sources, global_inner, terms, keys, values)

    p_in = lax.all_to_all(p_out, "ctx", 0, 0, tiled=True)
    p_before = lax.ppermute(own[-1], "ctx", up)
    p_after = lax.ppermute(own[0], "ctx", down)

    core = my_ctx % GLOB
    p_here = lax.dynamic_index_in_dim(p_in[:, CAP], global_owner[core], 0, keepdims=False)
    p_there = lax.ppermute(p_here, "ctx", [(i, i ^ 1) for i in range(ctx)])

    tile_owner = global_owner[jnp.minimum(my_ctx // (2 * PARTS), GLOB - 1)]
    kv_out = pl.pallas_call(
        add_tile,
        in_specs=[SMEM, ANY, VMEM],
        out_specs=ANY,
        out_shape=pltpu.HBM(kv_out.shape, BF16),
        input_output_aliases={1: 0},
        scratch_shapes=[pltpu.VMEM((ctx, ROWS, h), BF16), pltpu.SemaphoreType.DMA],
        compiler_params=PARAMS,
    )(tile_owner.reshape(1), kv_out, p_in)
    kv_out, p_before, p_after = lax.optimization_barrier((kv_out, p_before, p_after))
    kv_in = lax.all_to_all(kv_out, "ctx", 0, 0, tiled=True)

    tiles = pl.pallas_call(
        collect,
        in_specs=[SMEM, SMEM] + [VMEM] * 6,
        out_specs=VMEM,
        out_shape=jax.ShapeDtypeStruct((places, ROWS, 128), BF16),
        compiler_params=PARAMS,
    )(arrival, core.reshape(1), own, p_before, p_after, p_here, p_there, p_in)
    pair = [tiles, lax.ppermute(tiles, "head", [(i, i ^ 1) for i in range(heads)])]
    every = jnp.arange(D, dtype=jnp.int32)
    table_new = proj_table(step_codes[1], rank_ids, every)
    table_old = proj_table(step_codes[0], rank_ids, every)
    share = momentum.shape[1]
    carried = pl.pallas_call(
        carry,
        in_specs=[VMEM] * 3,
        out_specs=VMEM,
        out_shape=jax.ShapeDtypeStruct((8, RANK), F32),
        compiler_params=PARAMS,
    )(jnp.pad(momentum[0], ((0, 8 - share), (0, 0))), table_old, table_new)

    pair[1], carried = lax.optimization_barrier((pair[1], carried))
    all_tiles, all_heads = list(pair), [my_head, my_head ^ 1]
    for far in range(2, heads, 2):
        there = [(i, (i + far) % heads) for i in range(heads)]
        all_tiles += [lax.ppermute(t, "head", there) for t in pair]
        source = (my_head - far) % heads
        all_heads += [source, source ^ 1]

    edges = jnp.stack([my_ctx == 0, my_ctx == ctx - 1]).astype(jnp.int32)
    unroll = 8
    wide = pl.BlockSpec((unroll * BLK, GROUP * h), lambda i: (i, 0))
    queries, d_attn = (pltpu.with_memory_space_constraint(x, pltpu.HBM) for x in (queries, d_attn))
    dq, grad = pl.pallas_call(
        attend,
        grid=(blocks // unroll,),
        in_specs=[SMEM] * 3 + [wide] * 2 + [VMEM] * (5 + heads) + [ANY] * 2,
        out_specs=[wide, VMEM],
        out_shape=[
            jax.ShapeDtypeStruct((tokens, GROUP * h), BF16),
            pltpu.HBM((ctx, 2 * share, 128), F32),
        ],
        scratch_shapes=[
            pltpu.VMEM((tokens + 2 * BLK, h), BF16),
            pltpu.VMEM((tokens + 2 * BLK, h), BF16),
            pltpu.VMEM((GLOB * BLK, h), BF16),
            pltpu.VMEM((GLOB * BLK, h), BF16),
            pltpu.VMEM((tokens + 2 * BLK, 2 * h), F32),
            pltpu.VMEM((GLOB * BLK, 2 * h), F32),
            pltpu.VMEM((PARTS, places, ROWS, 2 * h), BF16),
            pltpu.VMEM((2, 2 * h, 128), F32),
        ],
        compiler_params=LARGE,
    )(
        arrival, edges, jnp.stack(all_heads), queries, d_attn, keys, values, kv_before, kv_after, kv_in,
        *all_tiles, table_new, carried,
    )
    grad = lax.all_to_all(grad, "ctx", 0, 0, tiled=True)
    new_momentum, weight_step = pl.pallas_call(
        functools.partial(finish, 1.0 / math.sqrt(tokens * ctx)),
        in_specs=[VMEM] * 3,
        out_specs=[VMEM] * 2,
        out_shape=[
            jax.ShapeDtypeStruct((share, RANK), F32),
            jax.ShapeDtypeStruct((share, D), F32),
        ],
        compiler_params=PARAMS,
    )(grad, carried, table_new)
    return dq, new_momentum[None], weight_step[None]


def solution(mesh):
    in_specs = (
        P("ctx", "head"),
        P("ctx", "head"),
        P("ctx", "head"),
        P("ctx", "head"),
        P("ctx", "head"),
        P(),
        P(),
        P(),
        P("head", "ctx", None),
    )
    out_specs = (P("ctx", "head"), P("head", "ctx", None), P("head", "ctx", None))
    return jax.shard_map(local, mesh=mesh, in_specs=in_specs, out_specs=out_specs, check_vma=False)
```
